32 devices in a mesh: pair: 2 (over y), section: 4 (over z), dp: 4 (over x, core).
Axes of the slice: x: 2, y: 2, z: 4, core: 2. Of those that a mesh axis runs over, the one named last changes fastest.
Arguments:
- grads: float32 [8, 4, 8, 7168], P(('section', 'pair'), 'dp'), parts along dimension 0, may hold values from -6 to 6
- master: float32 [32, 7168], P(('section', 'pair', 'dp')), parts along dimension 0, may hold values from -6 to 6
- moment: float32 [32, 7168], P(('section', 'pair', 'dp')), parts along dimension 0, may hold values from -12 to 12
- second: float32 [32, 7168], P(('section', 'pair', 'dp')), parts along dimension 0, may hold values from 0.5 to 50
- step: int32 [4], P('section'), parts along dimension 0, may hold values from 1 to 8
Outputs:
- new_master: float32 [32, 7168], P(('section', 'pair', 'dp')), parts along dimension 0
- new_moment: float32 [32, 7168], P(('section', 'pair', 'dp')), parts along dimension 0
- new_second: float32 [32, 7168], P(('section', 'pair', 'dp')), parts along dimension 0
- params: bfloat16 [32, 7168], P('section'), parts along dimension 0
The draws below stay inside these ranges and needn't reach their ends.
There are 4 independent parts, one for each index of `section`. The reference program is written for one: setup_inputs(seed, part) draws one part's arguments, and reference() takes and returns one part's arrays. A program takes and returns all parts, laid end to end along the dimension named above; each array names one. Nothing has to cross between parts.
All inputs are finite; a program needn't handle non-finite values.
Results may differ from the reference program's by a relative error of at most 0.0004.
Values may be sent and summed in bfloat16 or wider, within the bound.
No kernel may reach another device: no remote copies, remote signals or barrier semaphores. Data moves between devices by JAX's collectives and lax.ppermute only.
A program may use at most 64 MiB of HBM per device.

```python
import math
import jax
import jax.numpy as jnp
from jax import lax

D = 7168
ROWS = 8
N_PAIR = 2
N_DP = 4


def spiked(drawn, key, source, target, blocks, factor):
    owner, partner = [(jnp.arange(drawn.shape[dim]) // (drawn.shape[dim] // blocks)).reshape([-1 if axis == dim else 1 for axis in range(drawn.ndim)]) for dim in (source, target)]
    chosen = jax.random.permutation(key, blocks)[partner]
    strong = (owner == chosen) | (owner == (partner + blocks // 2) % blocks)
    return jnp.where(strong, factor * drawn, drawn)


def shard_levels(key, extent, shards, low, largest):
    loudness = 1.0
    for position, parts in shards:
        heights = jax.random.uniform(jax.random.fold_in(jax.random.fold_in(key, 6), position), (parts,), jnp.float32, low / len(shards), largest / len(shards))
        loudness = loudness * jnp.repeat(jnp.exp(heights), extent[position] // parts).reshape((-1,) + (1,) * (len(extent) - 1 - position))
    return loudness


def gaussian(stream_key, extent, scale, reach, cuts=(), held_as=jnp.bfloat16):
    factor_of = shard_levels(stream_key, extent, cuts, -0.22, 0.18) if cuts else 1.0
    array = jax.random.normal(stream_key, extent, jnp.float32) * scale * factor_of
    return jnp.minimum(jnp.maximum(array, -reach), reach).astype(held_as)


def bell_draw_with(key, extent, width, bound, split, heavy, kind=jnp.bfloat16):
    array = width * jax.random.normal(key, extent, jnp.float32)
    if split:
        array = array * shard_levels(key, extent, split, -0.22, 0.18)
    return jnp.clip(spiked(array, jax.random.fold_in(key, 3), *heavy), -bound, bound).astype(kind)


def setup_inputs(seed: int = 0, part: int = 0) -> dict:
    seeds = jax.random.split(jax.random.key(seed), 6)
    part_keys = jax.random.split(jax.random.fold_in(seeds[5], part), 6)
    grads = bell_draw_with(part_keys[0], (N_PAIR, N_DP, ROWS, D), 1.0, 6.0, ((0, 2), (1, 4)), (1, 2, 4, 2.0), jnp.float32)
    master = gaussian(part_keys[1], (ROWS, D), 1.0, 6.0, ((0, 8),), jnp.float32)
    moment = gaussian(part_keys[2], (ROWS, D), 2.0, 12.0, ((0, 8),), jnp.float32)
    second = jnp.clip(jnp.exp(math.log(50.0) - 4.6051702 * jax.random.uniform(part_keys[3], (ROWS, D), jnp.float32) ** shard_levels(part_keys[3], (ROWS, D), ((0, 8),), -0.2, 0.2)), 0.5, 50.0)
    step = jax.random.randint(part_keys[4], (1,), 1, 9).astype(jnp.int32)
    return dict(grads=grads, master=master, moment=moment, second=second, step=step)


def reference(grads, master, moment, second, step):
    total = lax.optimization_barrier(jnp.sum(grads.astype(jnp.float32), axis=(0, 1)))
    new_moment = 0.9 * moment + 0.1 * total
    new_second = 0.95 * second + 0.05 * total * total
    count = step[0].astype(jnp.float32)
    first_fix = 1.0 - jnp.power(jnp.float32(0.9), count)
    second_fix = 1.0 - jnp.power(jnp.float32(0.95), count)
    update = new_moment / first_fix / (jnp.sqrt(new_second / second_fix) + 1e-08) + 0.1 * master
    new_master = master - 0.03 * update
    return (new_master, new_moment, new_second, new_master.astype(jnp.bfloat16))
```

```python
import jax
import jax.numpy as jnp
from jax import lax
from jax.sharding import PartitionSpec as P

GROUP = ("pair", "dp")


def per_device(grads, master, moment, second, step):
    rows, width = grads.shape[2], grads.shape[3]
    own = master.shape[0]
    local = grads.reshape(rows // own, own, width)
    pieces = lax.all_to_all(local, GROUP, split_axis=0, concat_axis=0, tiled=True)
    total = jnp.sum(pieces, axis=0)
    new_moment = 0.9 * moment + 0.1 * total
    new_second = 0.95 * second + 0.05 * total * total
    count = step[0].astype(jnp.float32)
    first_fix = 1.0 - jnp.power(jnp.float32(0.9), count)
    second_fix = 1.0 - jnp.power(jnp.float32(0.95), count)
    update = new_moment / first_fix / (jnp.sqrt(new_second / second_fix) + 1e-08) + 0.1 * master
    new_master = master - 0.03 * update
    shard_params = new_master.astype(jnp.bfloat16)
    params = lax.all_gather(shard_params, GROUP, axis=0, tiled=True)
    return (new_master, new_moment, new_second, params)


def solution(mesh):
    placed = (
        P(("section", "pair"), "dp", None, None),
        P(("section", "pair", "dp"), None),
        P(("section", "pair", "dp"), None),
        P(("section", "pair", "dp"), None),
        P("section"),
    )
    return jax.shard_map(
        per_device,
        mesh=mesh,
        in_specs=placed,
        out_specs=(
            P(("section", "pair", "dp"), None),
            P(("section", "pair", "dp"), None),
            P(("section", "pair", "dp"), None),
            P("section", None),
        ),
        check_vma=False,
    )
```

```python
import jax
import jax.numpy as jnp
from jax import lax
from jax.sharding import PartitionSpec as P

GROUP = ("pair", "dp")


def gather_rows(row):
    size = lax.axis_size(GROUP)
    me = lax.axis_index(GROUP)
    pieces = [row]
    for k in range(1, size):
        pieces.append(lax.ppermute(row, GROUP, [(i, i ^ k) for i in range(size)]))
    stride = 1
    while stride < size:
        flip = (me // stride) % 2 == 1
        pieces = [jnp.where(flip, pieces[j ^ stride], pieces[j]) for j in range(size)]
        stride *= 2
    return jnp.concatenate(pieces, axis=0)


def per_device(grads, master, moment, second, step):
    rows, width = grads.shape[2], grads.shape[3]
    own = master.shape[0]
    local = grads.reshape(rows // own, own, width)
    pieces = lax.all_to_all(local, GROUP, split_axis=0, concat_axis=0, tiled=True)
    total = jnp.sum(pieces, axis=0)
    new_moment = 0.9 * moment + 0.1 * total
    new_second = 0.95 * second + 0.05 * total * total
    count = step[0].astype(jnp.float32)
    first_fix = 1.0 - jnp.power(jnp.float32(0.9), count)
    second_fix = 1.0 - jnp.power(jnp.float32(0.95), count)
    update = new_moment / first_fix / (jnp.sqrt(new_second / second_fix) + 1e-08) + 0.1 * master
    new_master = master - 0.03 * update
    shard_params = new_master.astype(jnp.bfloat16)
    params = gather_rows(shard_params)
    return (new_master, new_moment, new_second, params)


def solution(mesh):
    placed = (
        P(("section", "pair"), "dp", None, None),
        P(("section", "pair", "dp"), None),
        P(("section", "pair", "dp"), None),
        P(("section", "pair", "dp"), None),
        P("section"),
    )
    return jax.shard_map(
        per_device,
        mesh=mesh,
        in_specs=placed,
        out_specs=(
            P(("section", "pair", "dp"), None),
            P(("section", "pair", "dp"), None),
            P(("section", "pair", "dp"), None),
            P("section", None),
        ),
        check_vma=False,
    )
```

```python
import jax
import jax.numpy as jnp
from jax import lax
from jax.sharding import PartitionSpec as P

GROUP = ("pair", "dp")


def swap(array, bit):
    size = lax.axis_size(GROUP)
    return lax.ppermute(array, GROUP, [(i, i ^ bit) for i in range(size)])


def take(array, axis, index):
    return lax.dynamic_slice_in_dim(array, index, 1, axis)


def adam(total, master, moment, second, step):
    new_moment = 0.9 * moment + 0.1 * total
    new_second = 0.95 * second + 0.05 * total * total
    count = step[0].astype(jnp.float32)
    first_fix = 1.0 - jnp.power(jnp.float32(0.9), count)
    second_fix = 1.0 - jnp.power(jnp.float32(0.95), count)
    update = new_moment / first_fix / (jnp.sqrt(new_second / second_fix) + 1e-08) + 0.1 * master
    return master - 0.03 * update, new_moment, new_second


def in_order(first, mine, theirs):
    return jnp.where(first, mine, theirs), jnp.where(first, theirs, mine)


def per_device(grads, master, moment, second, step):
    rows, width = grads.shape[2], grads.shape[3]
    own = master.shape[0]
    pairs, shards = lax.axis_size("pair"), lax.axis_size("dp")
    pair, shard = lax.axis_index("pair"), lax.axis_index("dp")
    half = shards

    state = jnp.concatenate([master, moment, second], axis=0)
    other_state = swap(state, half)

    local = grads.reshape(rows, width)
    local = (local + swap(local, 1)).reshape(pairs, shards, own, width)
    bit, kept = 1, local.reshape(pairs, shards // 2, 2, own, width)
    kept = take(kept, 2, shard & 1)[:, :, 0]
    while kept.shape[1] > 1:
        bit *= 2
        split = kept.reshape(pairs, kept.shape[1] // 2, 2, own, width)
        mine = jnp.where((shard & bit) != 0, 1, 0)
        give = take(split, 2, 1 - mine)[:, :, 0]
        kept = take(split, 2, mine)[:, :, 0] + swap(give, bit)
    both = kept.reshape(pairs * own, width)
    both = both + swap(both, half)

    first = pair == 0
    mine, theirs = jnp.where(first, both[:own], both[own:]), jnp.where(first, both[own:], both[:own])
    new_master, new_moment, new_second = adam(mine, master, moment, second, step)
    other = other_state.reshape(3, own, width)
    other_master, _, _ = adam(theirs, other[0], other[1], other[2], step)

    params = [p.astype(jnp.bfloat16) for p in in_order(first, new_master, other_master)]
    params = jnp.concatenate(params, axis=0).reshape(pairs, 1, own, width)
    bit = shards // 2
    while bit >= 1:
        got = swap(params, bit)
        low = (shard & bit) == 0
        lo, hi = in_order(low, params, got)
        params = jnp.stack([lo, hi], axis=2).reshape(pairs, -1, own, width)
        bit //= 2
    return (new_master, new_moment, new_second, params.reshape(rows, width))


def solution(mesh):
    placed = (
        P(("section", "pair"), "dp", None, None),
        P(("section", "pair", "dp"), None),
        P(("section", "pair", "dp"), None),
        P(("section", "pair", "dp"), None),
        P("section"),
    )
    return jax.shard_map(
        per_device,
        mesh=mesh,
        in_specs=placed,
        out_specs=(
            P(("section", "pair", "dp"), None),
            P(("section", "pair", "dp"), None),
            P(("section", "pair", "dp"), None),
            P("section", None),
        ),
        check_vma=False,
    )
```

```python
import jax
import jax.numpy as jnp
from jax import lax
from jax.sharding import PartitionSpec as P

GROUP = ("pair", "dp")


def swap(array, bit):
    size = lax.axis_size(GROUP)
    return lax.ppermute(array, GROUP, [(i, i ^ bit) for i in range(size)])


def adam(total, master, moment, second, step):
    new_moment = 0.9 * moment + 0.1 * total
    new_second = 0.95 * second + 0.05 * total * total
    count = step[0].astype(jnp.float32)
    first_fix = 1.0 - jnp.power(jnp.float32(0.9), count)
    second_fix = 1.0 - jnp.power(jnp.float32(0.95), count)
    update = new_moment / first_fix / (jnp.sqrt(new_second / second_fix) + 1e-08) + 0.1 * master
    return master - 0.03 * update, new_moment, new_second


def in_order(first, mine, theirs):
    return jnp.where(first, mine, theirs), jnp.where(first, theirs, mine)


def per_device(grads, master, moment, second, step):
    rows, width = grads.shape[2], grads.shape[3]
    own = master.shape[0]
    size = rows // own
    core = lax.axis_index("dp") & 1
    chips = [list(range(c, size, 2)) for c in (0, 1)]

    local = grads.reshape(rows, width)
    local = (local + swap(local, 1)).reshape(size // 2, 2, own, width)
    mine = jnp.where(core == 0, local[:, 0], local[:, 1])
    pieces = lax.all_to_all(mine, GROUP, 0, 0, axis_index_groups=chips, tiled=True)
    total = jnp.sum(pieces, axis=0)
    new_master, new_moment, new_second = adam(total, master, moment, second, step)

    params = new_master.astype(jnp.bfloat16)
    params = jnp.concatenate(in_order(core == 0, params, swap(params, 1)), axis=0)
    params = lax.all_gather(params, GROUP, axis=0, axis_index_groups=chips, tiled=True)
    return (new_master, new_moment, new_second, params)


def solution(mesh):
    placed = (
        P(("section", "pair"), "dp", None, None),
        P(("section", "pair", "dp"), None),
        P(("section", "pair", "dp"), None),
        P(("section", "pair", "dp"), None),
        P("section"),
    )
    return jax.shard_map(
        per_device,
        mesh=mesh,
        in_specs=placed,
        out_specs=(
            P(("section", "pair", "dp"), None),
            P(("section", "pair", "dp"), None),
            P(("section", "pair", "dp"), None),
            P("section", None),
        ),
        check_vma=False,
    )
```

```python
import jax
import jax.numpy as jnp
from jax import lax
from jax.sharding import PartitionSpec as P

GROUP = ("pair", "dp")


def swap(array, bit):
    size = lax.axis_size(GROUP)
    return lax.ppermute(array, GROUP, [(i, i ^ bit) for i in range(size)])


def adam(total, master, moment, second, step):
    new_moment = 0.9 * moment + 0.1 * total
    new_second = 0.95 * second + 0.05 * total * total
    count = step[0].astype(jnp.float32)
    first_fix = 1.0 - jnp.power(jnp.float32(0.9), count)
    second_fix = 1.0 - jnp.power(jnp.float32(0.95), count)
    update = new_moment / first_fix / (jnp.sqrt(new_second / second_fix) + 1e-08) + 0.1 * master
    return master - 0.03 * update, new_moment, new_second


def in_order(first, mine, theirs):
    return jnp.where(first, mine, theirs), jnp.where(first, theirs, mine)


def half_of(array, flag):
    return in_order(flag, array[:, :, 0], array[:, :, 1])


def per_device(grads, master, moment, second, step):
    rows, width = grads.shape[2], grads.shape[3]
    own = master.shape[0]
    pairs, shards = lax.axis_size("pair"), lax.axis_size("dp")
    pair, shard = lax.axis_index("pair"), lax.axis_index("dp")
    low_core, low_near = (shard & 1) == 0, (shard & 2) == 0
    far = [1 << b for b in range(2, (shards - 1).bit_length())]

    local = grads.reshape(rows, width)
    local = local + swap(local, 1)
    state = swap(jnp.concatenate([master, moment, second], axis=0), shards)
    kept, _ = half_of(local.reshape(pairs, shards // 2, 2, own, width), low_core)
    kept = kept.reshape(pairs, shards // 4, 2, own, width)

    for bit in reversed(far):
        kept = kept.reshape(pairs, 2, -1, 2, own, width)
        mine, give = in_order((shard & bit) == 0, kept[:, 0], kept[:, 1])
        kept = mine + swap(give, bit)
    keep, give = half_of(kept.reshape(pairs, 1, 2, own, width), low_near)
    keep, give = keep.reshape(pairs * own, width), give.reshape(pairs * own, width)
    near, level, cross = swap(give, 2), swap(keep, shards), swap(give, shards | 2)
    both = (keep + near) + (level + cross)

    mine, theirs = in_order(pair == 0, both[:own], both[own:])
    new_master, new_moment, new_second = adam(mine, master, moment, second, step)
    other = state.reshape(3, own, width)
    other_master, _, _ = adam(theirs, other[0], other[1], other[2], step)

    params = jnp.concatenate([new_master, other_master], axis=0).astype(jnp.bfloat16)
    a, b, c, d = params, swap(params, 1), swap(params, 2), swap(params, 3)
    a, b = in_order(low_core, a, b)
    c, d = in_order(low_core, c, d)
    a, c = in_order(low_near, a, c)
    b, d = in_order(low_near, b, d)
    params = jnp.stack([p.reshape(pairs, own, width) for p in (a, b, c, d)], axis=1)
    for bit in far:
        got = swap(params, bit)
        params = jnp.concatenate(in_order((shard & bit) == 0, params, got), axis=1)
    params = jnp.concatenate(in_order(pair == 0, params[0], params[1]), axis=0)
    return (new_master, new_moment, new_second, params.reshape(rows, width))


def solution(mesh):
    placed = (
        P(("section", "pair"), "dp", None, None),
        P(("section", "pair", "dp"), None),
        P(("section", "pair", "dp"), None),
        P(("section", "pair", "dp"), None),
        P("section"),
    )
    return jax.shard_map(
        per_device,
        mesh=mesh,
        in_specs=placed,
        out_specs=(
            P(("section", "pair", "dp"), None),
            P(("section", "pair", "dp"), None),
            P(("section", "pair", "dp"), None),
            P("section", None),
        ),
        check_vma=False,
    )
```

```python
import functools

import jax
import jax.numpy as jnp
from jax import lax
from jax.experimental import pallas as pl
from jax.experimental.pallas import tpu as pltpu
from jax.sharding import PartitionSpec as P

GROUP = ("pair", "dp")
LANES = 128


def swap(array, bit):
    size = lax.axis_size(GROUP)
    return lax.ppermute(array, GROUP, [(i, i ^ bit) for i in range(size)])


def row_at(row, tiles, rows):
    sub = min(8, rows)
    return pl.ds((row // sub) * (tiles * sub) + row % sub, tiles, stride=sub)


def sum_kernel(pairs, shards, own, tiles, mine_ref, theirs_ref, keep_ref, give_ref):
    shard = lax.axis_index("dp")
    core, near = shard & 1, shard & 2
    rows = pairs * shards * own
    slot = 0
    for pair in range(pairs):
        for far in range(shards // 4):
            for o in range(own):
                for out_ref, bit in ((keep_ref, near), (give_ref, 2 - near)):
                    row = (pair * shards + far * 4 + bit + core) * own + o
                    at = row_at(row, tiles, rows)
                    out_ref[slot * tiles:(slot + 1) * tiles, :] = mine_ref[at, :] + theirs_ref[at, :]
                slot += 1


def adam(total, master, moment, second, count):
    new_moment = 0.9 * moment + 0.1 * total
    new_second = 0.95 * second + 0.05 * total * total
    first_fix = 1.0 - jnp.exp(count * jnp.log(jnp.full_like(count, 0.9)))
    second_fix = 1.0 - jnp.exp(count * jnp.log(jnp.full_like(count, 0.95)))
    update = new_moment / first_fix / (jnp.sqrt(new_second / second_fix) + 1e-08) + 0.1 * master
    return master - 0.03 * update, new_moment, new_second


def totals(size, sums):
    keep, near, level, cross = (s[...] for s in sums)
    both = (keep + near) + (level + cross)
    first = lax.axis_index("pair") == 0
    low, high = both[:size], both[size:]
    return jnp.where(first, low, high), jnp.where(first, high, low)


def params_kernel(size, step_ref, keep, near, level, cross, master, moment, second, state, out_ref):
    count = jnp.full((1, LANES), step_ref[0], jnp.int32).astype(jnp.float32)
    mine, theirs = totals(size, (keep, near, level, cross))
    a, _, _ = adam(mine, master[...], moment[...], second[...], count)
    b, _, _ = adam(theirs, state[:size], state[size:2 * size], state[2 * size:], count)
    out_ref[...] = jnp.concatenate([a, b], axis=0).astype(out_ref.dtype)


def own_kernel(size, step_ref, keep, near, level, cross, master, moment, second, m_ref, v_ref, s_ref):
    count = jnp.full((1, LANES), step_ref[0], jnp.int32).astype(jnp.float32)
    mine, _ = totals(size, (keep, near, level, cross))
    m_ref[...], v_ref[...], s_ref[...] = adam(mine, master[...], moment[...], second[...], count)


def order_kernel(pairs, shards, own, tiles, *refs):
    pieces, out_ref, scratch = refs[:4], refs[4], refs[5]
    pair, shard = lax.axis_index("pair"), lax.axis_index("dp") & 3
    rows = pairs * 4 * own
    for k in range(4):
        piece = pieces[k][...].astype(jnp.float32)
        for s in range(pairs):
            for o in range(own):
                row = ((pair ^ s) * 4 + (shard ^ k)) * own + o
                start = (s * own + o) * tiles
                scratch[row_at(row, tiles, rows), :] = piece[start:start + tiles]
    out_ref[...] = scratch[...].astype(out_ref.dtype)


def call(body, outs, *args, scratch=()):
    specs = [pl.BlockSpec(memory_space=pltpu.SMEM if a.dtype == jnp.int32 else pltpu.VMEM) for a in args]
    return pl.pallas_call(
        body,
        out_shape=outs,
        in_specs=specs,
        out_specs=jax.tree.map(lambda _: pl.BlockSpec(memory_space=pltpu.VMEM), outs),
        scratch_shapes=list(scratch),
    )(*args)


def per_device(grads, master, moment, second, step):
    rows, width = grads.shape[2], grads.shape[3]
    own, tiles = master.shape[0], width // LANES
    pairs, shards = lax.axis_size("pair"), lax.axis_size("dp")
    shard = lax.axis_index("dp")
    far = [1 << b for b in range(2, (shards - 1).bit_length())]
    size, f32 = own * tiles, jnp.float32
    shaped = jax.ShapeDtypeStruct

    master, moment, second = (a.reshape(size, LANES) for a in (master, moment, second))
    sub = min(8, rows)
    local = grads.reshape(rows // sub, sub, tiles, LANES).transpose(0, 2, 1, 3).reshape(rows * tiles, LANES)

    theirs = swap(local, 1)
    state = swap(jnp.concatenate([master, moment, second], axis=0), shards)
    half = shaped((pairs * (shards // 4) * size, LANES), f32)
    keep, give = call(
        functools.partial(sum_kernel, pairs, shards, own, tiles), (half, half), local, theirs)

    for bit in reversed(far):
        low = (shard & bit) == 0
        held = jnp.stack([keep, give]).reshape(2, pairs, 2, -1, LANES)
        mine = jnp.where(low, held[:, :, 0], held[:, :, 1])
        other = jnp.where(low, held[:, :, 1], held[:, :, 0])
        keep, give = (mine + swap(other, bit)).reshape(2, -1, LANES)

    near, cross = swap(give, 2), swap(give, shards | 2)
    keep, state = lax.optimization_barrier((keep, state))
    level = swap(keep, shards)
    sums = (keep, near, level, cross)

    params = call(
        functools.partial(params_kernel, size), shaped((pairs * size, LANES), jnp.bfloat16),
        step, *sums, master, moment, second, state)
    row = shaped((size, LANES), f32)
    news = call(
        functools.partial(own_kernel, size), (row, row, row), step, *sums, master, moment, second)

    pieces = [params, swap(params, 1), swap(params, 2), swap(params, 3)]
    block = pairs * 4 * size
    params = call(
        functools.partial(order_kernel, pairs, shards, own, tiles), shaped((block, LANES), jnp.bfloat16),
        *pieces, scratch=[pltpu.VMEM((block, LANES), f32)])
    near_rows = pairs * 4 * own
    sub = min(8, near_rows)
    params = params.reshape(near_rows // sub, tiles, sub, LANES).transpose(0, 2, 1, 3)
    params = params.reshape(pairs, 4 * own, width)
    for bit in far:
        low, got = (shard & bit) == 0, swap(params, bit)
        params = jnp.concatenate([jnp.where(low, params, got), jnp.where(low, got, params)], axis=1)
    return tuple(n.reshape(own, width) for n in news) + (params.reshape(rows, width),)


def solution(mesh):
    placed = (
        P(("section", "pair"), "dp", None, None),
        P(("section", "pair", "dp"), None),
        P(("section", "pair", "dp"), None),
        P(("section", "pair", "dp"), None),
        P("section"),
    )
    return jax.shard_map(
        per_device,
        mesh=mesh,
        in_specs=placed,
        out_specs=(
            P(("section", "pair", "dp"), None),
            P(("section", "pair", "dp"), None),
            P(("section", "pair", "dp"), None),
            P("section", None),
        ),
        check_vma=False,
    )
```

```python
import functools
import math

import jax
import jax.numpy as jnp
from jax import lax
from jax.experimental import pallas as pl
from jax.experimental.pallas import tpu as pltpu
from jax.sharding import PartitionSpec as P

GROUP = ("pair", "dp")
LANES = 128


def swap(array, bit):
    size = lax.axis_size(GROUP)
    return lax.ppermute(array, GROUP, [(i, i ^ bit) for i in range(size)])


def row_at(row, tiles, rows):
    sub = min(8, rows)
    return pl.ds((row // sub) * (tiles * sub) + row % sub, tiles, stride=sub)


def pick_kernel(pairs, shards, own, tiles, *refs):
    source_ref, added, (keep_ref, give_ref) = refs[0], refs[1:-2], refs[-2:]
    shard = lax.axis_index("dp")
    core, near = shard & 1, shard & 2
    rows = pairs * shards * own
    slot = 0
    for pair in range(pairs):
        for far in range(shards // 4):
            for o in range(own):
                to = slice(slot * tiles, (slot + 1) * tiles)
                for i, (out_ref, bit) in enumerate(((keep_ref, near), (give_ref, 2 - near))):
                    row = (pair * shards + far * 4 + bit + core) * own + o
                    picked = source_ref[row_at(row, tiles, rows), :]
                    out_ref[to, :] = picked + added[i][to, :] if added else picked
                slot += 1


def adam(total, master, moment, second, count):
    new_moment = 0.9 * moment + 0.1 * total
    new_second = 0.95 * second + 0.05 * total * total
    first_fix = 1.0 - jnp.exp(count * jnp.log(jnp.full_like(count, 0.9)))
    second_fix = 1.0 - jnp.exp(count * jnp.log(jnp.full_like(count, 0.95)))
    update = new_moment / first_fix / (jnp.sqrt(new_second / second_fix) + 1e-08) + 0.1 * master
    return master - 0.03 * update, new_moment, new_second


def totals(size, sums):
    keep, near, level, cross = (s[...] for s in sums)
    both = (keep + near) + (level + cross)
    first = lax.axis_index("pair") == 0
    low, high = both[:size], both[size:]
    return jnp.where(first, low, high), jnp.where(first, high, low)


def params_kernel(size, step_ref, keep, near, level, cross, master, moment, second, state, out_ref):
    count = jnp.full((1, LANES), step_ref[0], jnp.int32).astype(jnp.float32)
    mine, theirs = totals(size, (keep, near, level, cross))
    a, _, _ = adam(mine, master[...], moment[...], second[...], count)
    b, _, _ = adam(theirs, state[:size], state[size:2 * size], state[2 * size:], count)
    out_ref[...] = jnp.concatenate([a, b], axis=0).astype(out_ref.dtype)


def own_kernel(size, step_ref, keep, near, level, cross, master, moment, second, m_ref, v_ref, s_ref):
    count = jnp.full((1, LANES), step_ref[0], jnp.int32).astype(jnp.float32)
    mine, _ = totals(size, (keep, near, level, cross))
    m_ref[...], v_ref[...], s_ref[...] = adam(mine, master[...], moment[...], second[...], count)


def order_kernel(pairs, shards, own, tiles, *refs):
    pieces, out_ref, scratch = refs[:4], refs[4], refs[5]
    pair, shard = lax.axis_index("pair"), lax.axis_index("dp") & 3
    rows = pairs * 4 * own
    for k in range(4):
        piece = pieces[k][...].astype(jnp.float32)
        for s in range(pairs):
            for o in range(own):
                row = ((pair ^ s) * 4 + (shard ^ k)) * own + o
                start = (s * own + o) * tiles
                scratch[row_at(row, tiles, rows), :] = piece[start:start + tiles]
    out_ref[...] = scratch[...].astype(out_ref.dtype)


def call(body, outs, *args, scratch=()):
    held = sum(math.prod(a.shape) * a.dtype.itemsize for a in [*args, *jax.tree.leaves(outs)])
    specs = [pl.BlockSpec(memory_space=pltpu.SMEM if a.dtype == jnp.int32 else pltpu.VMEM) for a in args]
    return pl.pallas_call(
        body,
        out_shape=outs,
        in_specs=specs,
        out_specs=jax.tree.map(lambda _: pl.BlockSpec(memory_space=pltpu.VMEM), outs),
        scratch_shapes=list(scratch),
        compiler_params=pltpu.CompilerParams(vmem_limit_bytes=4 * held + (1 << 20)),
    )(*args)


def per_device(grads, master, moment, second, step):
    rows, width = grads.shape[2], grads.shape[3]
    own, tiles = master.shape[0], width // LANES
    pairs, shards = lax.axis_size("pair"), lax.axis_size("dp")
    shard = lax.axis_index("dp")
    far = [1 << b for b in range(2, (shards - 1).bit_length())]
    size, f32 = own * tiles, jnp.float32
    shaped = jax.ShapeDtypeStruct

    master, moment, second = (a.reshape(size, LANES) for a in (master, moment, second))
    sub = min(8, rows)
    local = grads.reshape(rows // sub, sub, tiles, LANES).transpose(0, 2, 1, 3).reshape(rows * tiles, LANES)

    theirs = swap(local, 1)
    state = swap(jnp.concatenate([master, moment, second], axis=0), shards)
    half = shaped((pairs * (shards // 4) * size, LANES), f32)
    pick = functools.partial(pick_kernel, pairs, shards, own, tiles)
    mine = call(pick, (half, half), local)
    keep, give = call(pick, (half, half), theirs, *mine)

    for bit in reversed(far):
        low = (shard & bit) == 0
        held = jnp.stack([keep, give]).reshape(2, pairs, 2, -1, LANES)
        mine = jnp.where(low, held[:, :, 0], held[:, :, 1])
        other = jnp.where(low, held[:, :, 1], held[:, :, 0])
        keep, give = (mine + swap(other, bit)).reshape(2, -1, LANES)

    near, cross = swap(give, 2), swap(give, shards | 2)
    level = swap(keep, shards)
    sums = (keep, near, level, cross)

    params = call(
        functools.partial(params_kernel, size), shaped((pairs * size, LANES), jnp.bfloat16),
        step, *sums, master, moment, second, state)
    row = shaped((size, LANES), f32)
    news = call(
        functools.partial(own_kernel, size), (row, row, row), step, *sums, master, moment, second)

    pieces = [params, swap(params, 1), swap(params, 2), swap(params, 3)]
    block = pairs * 4 * size
    params = call(
        functools.partial(order_kernel, pairs, shards, own, tiles), shaped((block, LANES), jnp.bfloat16),
        *pieces, scratch=[pltpu.VMEM((block, LANES), f32)])
    near_rows = pairs * 4 * own
    sub = min(8, near_rows)
    params = params.reshape(near_rows // sub, tiles, sub, LANES).transpose(0, 2, 1, 3)
    params = params.reshape(pairs, 4 * own, width)
    for bit in far:
        low, got = (shard & bit) == 0, swap(params, bit)
        params = jnp.concatenate([jnp.where(low, params, got), jnp.where(low, got, params)], axis=1)
    return tuple(n.reshape(own, width) for n in news) + (params.reshape(rows, width),)


def solution(mesh):
    placed = (
        P(("section", "pair"), "dp", None, None),
        P(("section", "pair", "dp"), None),
        P(("section", "pair", "dp"), None),
        P(("section", "pair", "dp"), None),
        P("section"),
    )
    return jax.shard_map(
        per_device,
        mesh=mesh,
        in_specs=placed,
        out_specs=(
            P(("section", "pair", "dp"), None),
            P(("section", "pair", "dp"), None),
            P(("section", "pair", "dp"), None),
            P("section", None),
        ),
        check_vma=False,
    )
```

```python
import functools
import math

import jax
import jax.numpy as jnp
from jax import lax
from jax.experimental import pallas as pl
from jax.experimental.pallas import tpu as pltpu
from jax.sharding import PartitionSpec as P

GROUP = ("pair", "dp")
LANES = 128


def swap(array, bit):
    size = lax.axis_size(GROUP)
    return lax.ppermute(array, GROUP, [(i, i ^ bit) for i in range(size)])


def row_at(row, tiles, rows):
    sub = min(8, rows)
    return pl.ds((row // sub) * (tiles * sub) + row % sub, tiles, stride=sub)


def my_rows(pairs, shards, own, tiles):
    shard = lax.axis_index("dp")
    core, near = shard & 1, shard & 2
    rows, slot = pairs * shards * own, 0
    for pair in range(pairs):
        for far in range(shards // 4):
            for o in range(own):
                first = pair * shards + far * 4 + core
                at = [row_at((first + bit) * own + o, tiles, rows) for bit in (near, 2 - near)]
                yield slice(slot * tiles, (slot + 1) * tiles), at
                slot += 1


def front_kernel(dims, local, master, moment, second, keep_ref, give_ref, state_ref, held, sems):
    size = master.shape[0]
    copies = [pltpu.make_async_copy(local, held, sems.at[3])]
    for i, source in enumerate((master, moment, second)):
        to = state_ref.at[pl.ds(i * size, size), :]
        copies.append(pltpu.make_async_copy(source, to, sems.at[i]))
    for copy in copies:
        copy.start()
    for copy in copies:
        copy.wait()
    for to, (mine, other) in my_rows(*dims):
        keep_ref[to, :] = held[mine, :]
        give_ref[to, :] = held[other, :]


def sum_kernel(dims, theirs, own_keep, own_give, give_ref, keep_ref):
    for to, (mine, other) in my_rows(*dims):
        keep_ref[to, :] = own_keep[to, :] + theirs[mine, :]
        give_ref[to, :] = own_give[to, :] + theirs[other, :]


def adam(total, master, moment, second, count):
    new_moment = 0.9 * moment + 0.1 * total
    new_second = 0.95 * second + 0.05 * total * total
    first_fix = 1.0 - jnp.exp(count * jnp.log(jnp.full_like(count, 0.9)))
    second_fix = 1.0 - jnp.exp(count * jnp.log(jnp.full_like(count, 0.95)))
    update = new_moment / first_fix / (jnp.sqrt(new_second / second_fix) + 1e-08) + 0.1 * master
    return master - 0.03 * update, new_moment, new_second


def totals(size, sums):
    cross, near, level, keep = (s[...] for s in sums)
    both = (keep + near) + (level + cross)
    first = lax.axis_index("pair") == 0
    low, high = both[:size], both[size:]
    return jnp.where(first, low, high), jnp.where(first, high, low)


def thirds(size, ref):
    return [ref[i * size:(i + 1) * size, :] for i in range(3)]


def params_kernel(size, step_ref, cross, near, level, keep, state, theirs_state, out_ref):
    count = jnp.full((1, LANES), step_ref[0], jnp.int32).astype(jnp.float32)
    mine, theirs = totals(size, (cross, near, level, keep))
    a, _, _ = adam(mine, *thirds(size, state), count)
    b, _, _ = adam(theirs, *thirds(size, theirs_state), count)
    out_ref[...] = jnp.concatenate([a, b], axis=0).astype(out_ref.dtype)


def own_kernel(size, step_ref, cross, near, level, keep, state, m_ref, v_ref, s_ref):
    count = jnp.full((1, LANES), step_ref[0], jnp.int32).astype(jnp.float32)
    mine, _ = totals(size, (cross, near, level, keep))
    m_ref[...], v_ref[...], s_ref[...] = adam(mine, *thirds(size, state), count)


def order_kernel(pairs, shards, own, tiles, *refs):
    pieces, out_ref, scratch = refs[3::-1], refs[4], refs[5]
    pair, shard = lax.axis_index("pair"), lax.axis_index("dp") & 3
    rows = pairs * 4 * own
    for k in range(4):
        piece = pieces[k][...].astype(jnp.float32)
        for s in range(pairs):
            for o in range(own):
                row = ((pair ^ s) * 4 + (shard ^ k)) * own + o
                start = (s * own + o) * tiles
                scratch[row_at(row, tiles, rows), :] = piece[start:start + tiles]
    out_ref[...] = scratch[...].astype(out_ref.dtype)


def call(body, outs, *args, hbm=False, scratch=()):
    space = pltpu.HBM if hbm else pltpu.VMEM
    specs = [pl.BlockSpec(memory_space=pltpu.SMEM if a.dtype == jnp.int32 else space) for a in args]
    held = sum(math.prod(a.shape) * a.dtype.itemsize for a in [*args, *jax.tree.leaves(outs)])
    return pl.pallas_call(
        body,
        out_shape=outs,
        in_specs=specs,
        out_specs=jax.tree.map(lambda _: pl.BlockSpec(memory_space=pltpu.VMEM), outs),
        scratch_shapes=list(scratch),
        compiler_params=pltpu.CompilerParams(vmem_limit_bytes=4 * held + (1 << 20)),
    )(*args)


def per_device(grads, master, moment, second, step):
    rows, width = grads.shape[2], grads.shape[3]
    own, tiles = master.shape[0], width // LANES
    pairs, shards = lax.axis_size("pair"), lax.axis_size("dp")
    shard = lax.axis_index("dp")
    far = [1 << b for b in range(2, (shards - 1).bit_length())]
    size, f32 = own * tiles, jnp.float32
    shaped = jax.ShapeDtypeStruct

    master, moment, second = (a.reshape(size, LANES) for a in (master, moment, second))
    sub = min(8, rows)
    local = grads.reshape(rows // sub, sub, tiles, LANES).transpose(0, 2, 1, 3).reshape(rows * tiles, LANES)

    dims = (pairs, shards, own, tiles)
    theirs = swap(local, 1)
    half = shaped((pairs * (shards // 4) * size, LANES), f32)
    keep, give, state = call(
        functools.partial(front_kernel, dims), (half, half, shaped((3 * size, LANES), f32)),
        *(pltpu.with_memory_space_constraint(a, pltpu.HBM) for a in (local, master, moment, second)), hbm=True,
        scratch=[pltpu.VMEM(local.shape, f32), pltpu.SemaphoreType.DMA((4,))])
    theirs_state = swap(state, shards)
    give, keep = call(functools.partial(sum_kernel, dims), (half, half), theirs, keep, give)

    for bit in reversed(far):
        low = (shard & bit) == 0
        held = jnp.stack([keep, give]).reshape(2, pairs, 2, -1, LANES)
        mine = jnp.where(low, held[:, :, 0], held[:, :, 1])
        other = jnp.where(low, held[:, :, 1], held[:, :, 0])
        keep, give = (mine + swap(other, bit)).reshape(2, -1, LANES)

    cross, near, level = swap(give, shards | 2), swap(give, 2), swap(keep, shards)
    sums = (cross, near, level, keep)

    params = call(
        functools.partial(params_kernel, size), shaped((pairs * size, LANES), jnp.bfloat16),
        step, *sums, state, theirs_state)
    row = shaped((size, LANES), f32)
    news = call(
        functools.partial(own_kernel, size), (row, row, row), step, *sums, state)

    pieces = [swap(params, bit) for bit in (3, 2, 1)] + [params]
    block = pairs * 4 * size
    params = call(
        functools.partial(order_kernel, pairs, shards, own, tiles), shaped((block, LANES), jnp.bfloat16),
        *pieces, scratch=[pltpu.VMEM((block, LANES), f32)])
    near_rows = pairs * 4 * own
    sub = min(8, near_rows)
    params = params.reshape(near_rows // sub, tiles, sub, LANES).transpose(0, 2, 1, 3)
    params = params.reshape(pairs, 4 * own, width)
    for bit in far:
        low, got = (shard & bit) == 0, swap(params, bit)
        params = jnp.concatenate([jnp.where(low, params, got), jnp.where(low, got, params)], axis=1)
    return tuple(n.reshape(own, width) for n in news) + (params.reshape(rows, width),)


def solution(mesh):
    placed = (
        P(("section", "pair"), "dp", None, None),
        P(("section", "pair", "dp"), None),
        P(("section", "pair", "dp"), None),
        P(("section", "pair", "dp"), None),
        P("section"),
    )
    return jax.shard_map(
        per_device,
        mesh=mesh,
        in_specs=placed,
        out_specs=(
            P(("section", "pair", "dp"), None),
            P(("section", "pair", "dp"), None),
            P(("section", "pair", "dp"), None),
            P("section", None),
        ),
        check_vma=False,
    )
```

```python
import functools
import math

import jax
import jax.numpy as jnp
from jax import lax
from jax.experimental import pallas as pl
from jax.experimental.pallas import tpu as pltpu
from jax.sharding import PartitionSpec as P

GROUP = ("pair", "dp")
LANES = 128


def send(array, bits, core_1_bits=None):
    size = lax.axis_size(GROUP)
    flip = (bits, bits if core_1_bits is None else core_1_bits)
    return lax.ppermute(array, GROUP, [(i, i ^ flip[i & 1]) for i in range(size)])


def row_at(row, tiles, rows):
    sub = min(8, rows)
    return pl.ds((row // sub) * (tiles * sub) + row % sub, tiles, stride=sub)


def place(slot, other):
    pair, shard = lax.axis_index("pair"), lax.axis_index("dp")
    core, near = shard & 1, (shard >> 1) & 1
    return pair ^ (slot * (1 - core)) ^ (other * core), near ^ (slot * core) ^ (other * (1 - core))


def my_rows(shards, own, tiles):
    core = lax.axis_index("dp") & 1
    rows, i = 2 * shards * own, 0
    for slot in range(2):
        kept, given = place(slot, 0), place(slot, 1)
        for far in range(shards // 4):
            for o in range(own):
                at = [
                    row_at((pair * shards + far * 4 + near * 2 + core) * own + o, tiles, rows)
                    for pair, near in (kept, given)
                ]
                yield slice(i * tiles, (i + 1) * tiles), at
                i += 1


def front_kernel(dims, local, master, moment, second, keep_ref, give_ref, state_ref, held, sems):
    size = master.shape[0]
    copies = [pltpu.make_async_copy(local, held, sems.at[3])]
    for i, source in enumerate((master, moment, second)):
        to = state_ref.at[pl.ds(i * size, size), :]
        copies.append(pltpu.make_async_copy(source, to, sems.at[i]))
    for copy in copies:
        copy.start()
    for copy in copies:
        copy.wait()
    for to, (mine, other) in my_rows(*dims):
        keep_ref[to, :] = held[mine, :]
        give_ref[to, :] = held[other, :]


def sum_kernel(dims, theirs, own_keep, own_give, give_ref, keep_ref):
    for to, (mine, other) in my_rows(*dims):
        keep_ref[to, :] = own_keep[to, :] + theirs[mine, :]
        give_ref[to, :] = own_give[to, :] + theirs[other, :]


def adam(total, master, moment, second, count):
    new_moment = 0.9 * moment + 0.1 * total
    new_second = 0.95 * second + 0.05 * total * total
    first_fix = 1.0 - jnp.exp(count * jnp.log(jnp.full_like(count, 0.9)))
    second_fix = 1.0 - jnp.exp(count * jnp.log(jnp.full_like(count, 0.95)))
    update = new_moment / first_fix / (jnp.sqrt(new_second / second_fix) + 1e-08) + 0.1 * master
    return master - 0.03 * update, new_moment, new_second


def totals(size, sums):
    cross, near, level, keep = (s[...] for s in sums)
    flip = lambda rows: (rows[size:], rows[:size])
    return [
        (c + n) + (l + k)
        for c, n, l, k in zip(flip(cross), flip(near)[::-1], flip(level), flip(keep)[::-1])
    ]


def thirds(size, ref):
    return [ref[i * size:(i + 1) * size, :] for i in range(3)]


def params_kernel(size, step_ref, cross, near, level, keep, state, theirs_state, out_ref):
    count = jnp.full((1, LANES), step_ref[0], jnp.int32).astype(jnp.float32)
    mine, theirs = totals(size, (cross, near, level, keep))
    a, _, _ = adam(mine, *thirds(size, state), count)
    b, _, _ = adam(theirs, *thirds(size, theirs_state), count)
    out_ref[...] = jnp.concatenate([a, b], axis=0).astype(out_ref.dtype)


def own_kernel(size, step_ref, cross, near, level, keep, state, m_ref, v_ref, s_ref):
    count = jnp.full((1, LANES), step_ref[0], jnp.int32).astype(jnp.float32)
    mine, _ = totals(size, (cross, near, level, keep))
    m_ref[...], v_ref[...], s_ref[...] = adam(mine, *thirds(size, state), count)


def order_kernel(own, tiles, *refs):
    pieces, out_ref, scratch = refs[:4], refs[4], refs[5]
    pair, shard = lax.axis_index("pair"), lax.axis_index("dp")
    core, near = shard & 1, (shard >> 1) & 1
    sources = (
        (pair ^ (1 - core), near ^ core, core ^ 1),
        (pair ^ core, near ^ (1 - core), core),
        (pair, near, core ^ 1),
        (pair, near, core),
    )
    for ref, (p, n, c) in zip(pieces, sources):
        piece = ref[...].astype(jnp.float32)
        for slot in range(2):
            for o in range(own):
                row = ((p ^ (slot * (1 - c))) * 4 + (n ^ (slot * c)) * 2 + c) * own + o
                start = (slot * own + o) * tiles
                scratch[row_at(row, tiles, 8 * own), :] = piece[start:start + tiles]
    out_ref[...] = scratch[...].astype(out_ref.dtype)


def call(body, outs, *args, hbm=False, scratch=()):
    space = pltpu.HBM if hbm else pltpu.VMEM
    specs = [pl.BlockSpec(memory_space=pltpu.SMEM if a.dtype == jnp.int32 else space) for a in args]
    held = sum(math.prod(a.shape) * a.dtype.itemsize for a in [*args, *jax.tree.leaves(outs)])
    return pl.pallas_call(
        body,
        out_shape=outs,
        in_specs=specs,
        out_specs=jax.tree.map(lambda _: pl.BlockSpec(memory_space=pltpu.VMEM), outs),
        scratch_shapes=list(scratch),
        compiler_params=pltpu.CompilerParams(vmem_limit_bytes=4 * held + (1 << 20)),
    )(*args)


def per_device(grads, master, moment, second, step):
    rows, width = grads.shape[2], grads.shape[3]
    own, tiles = master.shape[0], width // LANES
    shards = lax.axis_size("dp")
    shard = lax.axis_index("dp")
    far = [1 << b for b in range(2, (shards - 1).bit_length())]
    size, f32 = own * tiles, jnp.float32
    shaped = jax.ShapeDtypeStruct

    master, moment, second = (a.reshape(size, LANES) for a in (master, moment, second))
    sub = min(8, rows)
    local = grads.reshape(rows // sub, sub, tiles, LANES).transpose(0, 2, 1, 3).reshape(rows * tiles, LANES)

    dims = (shards, own, tiles)
    theirs = send(local, 1)
    half = shaped((shards // 2 * size, LANES), f32)
    keep, give, state = call(
        functools.partial(front_kernel, dims), (half, half, shaped((3 * size, LANES), f32)),
        *(pltpu.with_memory_space_constraint(a, pltpu.HBM) for a in (local, master, moment, second)), hbm=True,
        scratch=[pltpu.VMEM(local.shape, f32), pltpu.SemaphoreType.DMA((4,))])
    theirs_state = send(state, shards, 2)
    give, keep = call(functools.partial(sum_kernel, dims), (half, half), theirs, keep, give)

    for bit in reversed(far):
        low = (shard & bit) == 0
        held = jnp.stack([keep, give]).reshape(2, 2, 2, -1, LANES)
        mine = jnp.where(low, held[:, :, 0], held[:, :, 1])
        other = jnp.where(low, held[:, :, 1], held[:, :, 0])
        keep, give = (mine + send(other, bit)).reshape(2, -1, LANES)

    cross, near, level = send(give, shards | 2), send(give, 2, shards), send(keep, shards, 2)
    sums = (cross, near, level, keep)

    params = call(
        functools.partial(params_kernel, size), shaped((2 * size, LANES), jnp.bfloat16),
        step, *sums, state, theirs_state)
    row = shaped((size, LANES), f32)
    news = call(
        functools.partial(own_kernel, size), (row, row, row), step, *sums, state)

    pieces = [send(params, 3, shards | 1), send(params, 2, shards), send(params, 1), params]
    block, sub = 8 * own, min(8, 8 * own)
    params = call(
        functools.partial(order_kernel, own, tiles), shaped((block * tiles, LANES), jnp.bfloat16),
        *pieces, scratch=[pltpu.VMEM((block * tiles, LANES), f32)])
    params = params.reshape(block // sub, tiles, sub, LANES).transpose(0, 2, 1, 3).reshape(2, 4 * own, width)
    for bit in far:
        low, got = (shard & bit) == 0, send(params, bit)
        params = jnp.concatenate([jnp.where(low, params, got), jnp.where(low, got, params)], axis=1)
    return tuple(n.reshape(own, width) for n in news) + (params.reshape(rows, width),)


def solution(mesh):
    placed = (
        P(("section", "pair"), "dp", None, None),
        P(("section", "pair", "dp"), None),
        P(("section", "pair", "dp"), None),
        P(("section", "pair", "dp"), None),
        P("section"),
    )
    return jax.shard_map(
        per_device,
        mesh=mesh,
        in_specs=placed,
        out_specs=(
            P(("section", "pair", "dp"), None),
            P(("section", "pair", "dp"), None),
            P(("section", "pair", "dp"), None),
            P("section", None),
        ),
        check_vma=False,
    )
```

```python
import functools
import math

import jax
import jax.numpy as jnp
from jax import lax
from jax.experimental import pallas as pl
from jax.experimental.pallas import tpu as pltpu
from jax.sharding import PartitionSpec as P

GROUP = ("pair", "dp")
LANES = 128


def send(array, bits, core_1_bits=None):
    size = lax.axis_size(GROUP)
    flip = (bits, bits if core_1_bits is None else core_1_bits)
    return lax.ppermute(array, GROUP, [(i, i ^ flip[i & 1]) for i in range(size)])


def row_at(row, tiles, rows):
    sub = min(8, rows)
    return pl.ds((row // sub) * (tiles * sub) + row % sub, tiles, stride=sub)


def place(slot, other):
    pair, shard = lax.axis_index("pair"), lax.axis_index("dp")
    core, near = shard & 1, (shard >> 1) & 1
    return pair ^ (slot * (1 - core)) ^ (other * core), near ^ (slot * core) ^ (other * (1 - core))


def my_rows(shards, own, tiles):
    core, i = lax.axis_index("dp") & 1, 0
    for slot in range(2):
        kept, given = place(slot, 0), place(slot, 1)
        for far in range(shards // 4):
            for o in range(own):
                yield pl.ds(i * tiles, tiles), [
                    (pair * shards + far * 4 + near * 2 + core) * own + o for pair, near in (kept, given)
                ]
                i += 1


def front_kernel(dims, local, master, moment, second, keep_ref, give_ref, state_ref, sems):
    size, tiles, sub = master.shape[0], dims[2], local.shape[1]
    copies = []
    for i, source in enumerate((master, moment, second)):
        copies.append((source, state_ref.at[pl.ds(i * size, size)]))
    for to, rows in my_rows(*dims):
        for row, out_ref in zip(rows, (keep_ref, give_ref)):
            block = pl.ds((row // sub) * tiles, tiles)
            copies.append((local.at[block, row % sub], out_ref.at[to]))
    copies = [pltpu.make_async_copy(*c, sems.at[i]) for i, c in enumerate(copies)]
    for copy in copies:
        copy.start()
    for copy in copies:
        copy.wait()


def sum_kernel(dims, theirs, own_keep, own_give, cross_ref, near_ref, level_ref, keep_ref):
    tiles, rows = dims[2], 2 * dims[0] * dims[1]
    for to, (kept, given) in my_rows(*dims):
        keep = own_keep[to, :] + theirs[row_at(kept, tiles, rows), :]
        keep_ref[to, :] = keep
        level_ref[to, :] = keep
        give = own_give[to, :] + theirs[row_at(given, tiles, rows), :]
        cross_ref[to, :] = give
        near_ref[to, :] = give


def adam(total, master, moment, second, count):
    new_moment = 0.9 * moment + 0.1 * total
    new_second = 0.95 * second + 0.05 * total * total
    first_fix = 1.0 - jnp.exp(count * jnp.log(jnp.full_like(count, 0.9)))
    second_fix = 1.0 - jnp.exp(count * jnp.log(jnp.full_like(count, 0.95)))
    update = new_moment / first_fix / (jnp.sqrt(new_second / second_fix) + 1e-08) + 0.1 * master
    return master - 0.03 * update, new_moment, new_second


def totals(size, sums):
    cross, near, level, keep = (s[...] for s in sums)
    flip = lambda rows: (rows[size:], rows[:size])
    return [
        (c + n) + (l + k)
        for c, n, l, k in zip(flip(cross), flip(near)[::-1], flip(level), flip(keep)[::-1])
    ]


def thirds(size, ref):
    return [ref[i * size:(i + 1) * size, :] for i in range(3)]


def params_kernel(size, step_ref, cross, near, level, keep, state, theirs_state, out_ref):
    count = jnp.full((1, LANES), step_ref[0], jnp.int32).astype(jnp.float32)
    mine, theirs = totals(size, (cross, near, level, keep))
    a, _, _ = adam(mine, *thirds(size, state), count)
    b, _, _ = adam(theirs, *thirds(size, theirs_state), count)
    out_ref[...] = jnp.concatenate([a, b], axis=0).astype(out_ref.dtype)


def own_kernel(size, step_ref, cross, near, level, keep, state, m_ref, v_ref, s_ref):
    count = jnp.full((1, LANES), step_ref[0], jnp.int32).astype(jnp.float32)
    mine, _ = totals(size, (cross, near, level, keep))
    m_ref[...], v_ref[...], s_ref[...] = adam(mine, *thirds(size, state), count)


def order_kernel(own, tiles, *refs):
    pieces, out_ref, scratch = refs[:4], refs[4], refs[5]
    pair, shard = lax.axis_index("pair"), lax.axis_index("dp")
    core, near = shard & 1, (shard >> 1) & 1
    sources = (
        (pair ^ (1 - core), near ^ core, core ^ 1),
        (pair ^ core, near ^ (1 - core), core),
        (pair, near, core ^ 1),
        (pair, near, core),
    )
    for ref, (p, n, c) in zip(pieces, sources):
        piece = ref[...].astype(jnp.float32)
        for slot in range(2):
            for o in range(own):
                row = ((p ^ (slot * (1 - c))) * 4 + (n ^ (slot * c)) * 2 + c) * own + o
                start = (slot * own + o) * tiles
                scratch[row_at(row, tiles, 8 * own), :] = piece[start:start + tiles]
    out_ref[...] = scratch[...].astype(out_ref.dtype)


def call(body, outs, *args, hbm=False, scratch=()):
    space = pltpu.HBM if hbm else pltpu.VMEM
    specs = [pl.BlockSpec(memory_space=pltpu.SMEM if a.dtype == jnp.int32 else space) for a in args]
    held = sum(math.prod(a.shape) * a.dtype.itemsize for a in [*args, *jax.tree.leaves(outs)])
    return pl.pallas_call(
        body,
        out_shape=outs,
        in_specs=specs,
        out_specs=jax.tree.map(lambda _: pl.BlockSpec(memory_space=pltpu.VMEM), outs),
        scratch_shapes=list(scratch),
        compiler_params=pltpu.CompilerParams(vmem_limit_bytes=4 * held + (1 << 20)),
    )(*args)


def per_device(grads, master, moment, second, step):
    rows, width = grads.shape[2], grads.shape[3]
    own, tiles = master.shape[0], width // LANES
    shards = lax.axis_size("dp")
    shard = lax.axis_index("dp")
    far = [1 << b for b in range(2, (shards - 1).bit_length())]
    size, f32 = own * tiles, jnp.float32
    shaped = jax.ShapeDtypeStruct

    master, moment, second = (a.reshape(size, LANES) for a in (master, moment, second))
    sub = min(8, rows)
    local = grads.reshape(rows // sub, sub, tiles, LANES).transpose(0, 2, 1, 3).reshape(rows * tiles, LANES)

    dims = (shards, own, tiles)
    theirs = send(local, 1)
    half = shaped((shards // 2 * size, LANES), f32)
    blocks = local.reshape(rows // sub * tiles, sub, 1, LANES)
    flat = [a.reshape(size, 1, LANES) for a in (master, moment, second)]
    picked = shaped((half.shape[0], 1, LANES), f32)
    keep, give, state = (a.reshape(-1, LANES) for a in call(
        functools.partial(front_kernel, dims), (picked, picked, shaped((3 * size, 1, LANES), f32)),
        *(pltpu.with_memory_space_constraint(a, pltpu.HBM) for a in (blocks, *flat)), hbm=True,
        scratch=[pltpu.SemaphoreType.DMA((3 + 2 * (half.shape[0] // tiles),))]))
    theirs_state = send(state, shards, 2)
    to_cross, to_near, to_level, keep = call(functools.partial(sum_kernel, dims), (half, half, half, half), theirs, keep, give)

    for bit in reversed(far):
        low = (shard & bit) == 0
        held = jnp.stack([keep, to_near]).reshape(2, 2, 2, -1, LANES)
        mine = jnp.where(low, held[:, :, 0], held[:, :, 1])
        other = jnp.where(low, held[:, :, 1], held[:, :, 0])
        keep, to_near = (mine + send(other, bit)).reshape(2, -1, LANES)
        to_cross, to_level = to_near, keep

    cross, near, level = send(to_cross, shards | 2), send(to_near, 2, shards), send(to_level, shards, 2)
    sums = (cross, near, level, keep)

    params = call(
        functools.partial(params_kernel, size), shaped((2 * size, LANES), jnp.bfloat16),
        step, *sums, state, theirs_state)
    row = shaped((size, LANES), f32)
    news = call(
        functools.partial(own_kernel, size), (row, row, row), step, *sums, state)

    pieces = [send(params, 3, shards | 1), send(params, 2, shards), send(params, 1), params]
    block, sub = 8 * own, min(8, 8 * own)
    params = call(
        functools.partial(order_kernel, own, tiles), shaped((block * tiles, LANES), jnp.bfloat16),
        *pieces, scratch=[pltpu.VMEM((block * tiles, LANES), f32)])
    params = params.reshape(block // sub, tiles, sub, LANES).transpose(0, 2, 1, 3).reshape(2, 4 * own, width)
    for bit in far:
        low, got = (shard & bit) == 0, send(params, bit)
        params = jnp.concatenate([jnp.where(low, params, got), jnp.where(low, got, params)], axis=1)
    return tuple(n.reshape(own, width) for n in news) + (params.reshape(rows, width),)


def solution(mesh):
    placed = (
        P(("section", "pair"), "dp", None, None),
        P(("section", "pair", "dp"), None),
        P(("section", "pair", "dp"), None),
        P(("section", "pair", "dp"), None),
        P("section"),
    )
    return jax.shard_map(
        per_device,
        mesh=mesh,
        in_specs=placed,
        out_specs=(
            P(("section", "pair", "dp"), None),
            P(("section", "pair", "dp"), None),
            P(("section", "pair", "dp"), None),
            P("section", None),
        ),
        check_vma=False,
    )
```

```python
import functools
import math

import jax
import jax.numpy as jnp
from jax import lax
from jax.experimental import pallas as pl
from jax.experimental.pallas import tpu as pltpu
from jax.sharding import PartitionSpec as P

GROUP = ("pair", "dp")
LANES = 128


def send(array, bits, core_1_bits=None):
    size = lax.axis_size(GROUP)
    flip = (bits, bits if core_1_bits is None else core_1_bits)
    return lax.ppermute(array, GROUP, [(i, i ^ flip[i & 1]) for i in range(size)])


def row_at(row, tiles, rows):
    sub = min(8, rows)
    return pl.ds((row // sub) * (tiles * sub) + row % sub, tiles, stride=sub)


def place(core, slot, other):
    pair, near = lax.axis_index("pair"), (lax.axis_index("dp") >> 1) & 1
    return pair ^ (slot * (1 - core)) ^ (other * core), near ^ (slot * core) ^ (other * (1 - core))


def my_rows(shards, own, tiles):
    core, i = lax.axis_index("dp") & 1, 0
    for slot in range(2):
        places = [(*place(c, slot, other), c) for c, other in ((core, 0), (1 - core, 0), (1 - core, 1))]
        for far in range(shards // 4):
            for o in range(own):
                yield pl.ds(i * tiles, tiles), [
                    (pair * shards + far * 4 + near * 2 + c) * own + o for pair, near, c in places
                ]
                i += 1


def front_kernel(dims, local, master, moment, second, keep_ref, level_ref, give_ref, state_ref, sems):
    size, tiles, sub = master.shape[0], dims[2], local.shape[1]
    copies = []
    for i, source in enumerate((master, moment, second)):
        copies.append((source, state_ref.at[pl.ds(i * size, size)]))
    for to, rows in my_rows(*dims):
        for row, out_ref in zip(rows, (keep_ref, level_ref, give_ref)):
            block = pl.ds((row // sub) * tiles, tiles)
            copies.append((local.at[block, row % sub], out_ref.at[to]))
    copies = [pltpu.make_async_copy(*c, sems.at[i]) for i, c in enumerate(copies)]
    for copy in copies:
        copy.start()
    for copy in copies:
        copy.wait()


def sum_kernel(dims, theirs, own_keep, own_level, own_give, cross_ref, near_ref, level_ref, keep_ref):
    tiles, rows = dims[2], 2 * dims[0] * dims[1]
    for to, (kept, level, given) in my_rows(*dims):
        keep_ref[to, :] = own_keep[to, :] + theirs[row_at(kept, tiles, rows), :]
        level_ref[to, :] = own_level[to, :] + theirs[row_at(level, tiles, rows), :]
        give = own_give[to, :] + theirs[row_at(given, tiles, rows), :]
        cross_ref[to, :] = give
        near_ref[to, :] = give


def adam(total, master, moment, second, count):
    new_moment = 0.9 * moment + 0.1 * total
    new_second = 0.95 * second + 0.05 * total * total
    first_fix = 1.0 - jnp.exp(count * jnp.log(jnp.full_like(count, 0.9)))
    second_fix = 1.0 - jnp.exp(count * jnp.log(jnp.full_like(count, 0.95)))
    update = new_moment / first_fix / (jnp.sqrt(new_second / second_fix) + 1e-08) + 0.1 * master
    return master - 0.03 * update, new_moment, new_second


def totals(size, sums):
    cross, near, level, keep = (s[...] for s in sums)
    flip = lambda rows: (rows[size:], rows[:size])
    return [
        (c + n) + (l + k)
        for c, n, l, k in zip(flip(cross), flip(near)[::-1], flip(level), flip(keep)[::-1])
    ]


def thirds(size, ref):
    return [ref[i * size:(i + 1) * size, :] for i in range(3)]


def params_kernel(size, step_ref, cross, near, level, keep, state, theirs_state, out_ref):
    count = jnp.full((1, LANES), step_ref[0], jnp.int32).astype(jnp.float32)
    mine, theirs = totals(size, (cross, near, level, keep))
    a, _, _ = adam(mine, *thirds(size, state), count)
    b, _, _ = adam(theirs, *thirds(size, theirs_state), count)
    out_ref[...] = jnp.concatenate([a, b], axis=0).astype(out_ref.dtype)


def own_kernel(size, step_ref, cross, near, level, keep, state, m_ref, v_ref, s_ref):
    count = jnp.full((1, LANES), step_ref[0], jnp.int32).astype(jnp.float32)
    mine, _ = totals(size, (cross, near, level, keep))
    m_ref[...], v_ref[...], s_ref[...] = adam(mine, *thirds(size, state), count)


def order_kernel(own, tiles, *refs):
    pieces, out_ref, scratch = refs[:4], refs[4], refs[5]
    pair, shard = lax.axis_index("pair"), lax.axis_index("dp")
    core, near = shard & 1, (shard >> 1) & 1
    sources = (
        (pair ^ core, near ^ (1 - core), core),
        (pair ^ (1 - core), near ^ core, core ^ 1),
        (pair, near, core ^ 1),
        (pair, near, core),
    )
    for ref, (p, n, c) in zip(pieces, sources):
        piece = ref[...].astype(jnp.float32)
        for slot in range(2):
            for o in range(own):
                row = ((p ^ (slot * (1 - c))) * 4 + (n ^ (slot * c)) * 2 + c) * own + o
                start = (slot * own + o) * tiles
                scratch[row_at(row, tiles, 8 * own), :] = piece[start:start + tiles]
    out_ref[...] = scratch[...].astype(out_ref.dtype)


def call(body, outs, *args, hbm=False, scratch=()):
    space = pltpu.HBM if hbm else pltpu.VMEM
    specs = [pl.BlockSpec(memory_space=pltpu.SMEM if a.dtype == jnp.int32 else space) for a in args]
    held = sum(math.prod(a.shape) * a.dtype.itemsize for a in [*args, *jax.tree.leaves(outs)])
    return pl.pallas_call(
        body,
        out_shape=outs,
        in_specs=specs,
        out_specs=jax.tree.map(lambda _: pl.BlockSpec(memory_space=pltpu.VMEM), outs),
        scratch_shapes=list(scratch),
        compiler_params=pltpu.CompilerParams(vmem_limit_bytes=4 * held + (1 << 20)),
    )(*args)


def per_device(grads, master, moment, second, step):
    rows, width = grads.shape[2], grads.shape[3]
    own, tiles = master.shape[0], width // LANES
    shards = lax.axis_size("dp")
    shard = lax.axis_index("dp")
    far = [1 << b for b in range(2, (shards - 1).bit_length())]
    size, f32 = own * tiles, jnp.float32
    shaped = jax.ShapeDtypeStruct

    master, moment, second = (a.reshape(size, LANES) for a in (master, moment, second))
    sub = min(8, rows)
    local = grads.reshape(rows // sub, sub, tiles, LANES).transpose(0, 2, 1, 3).reshape(rows * tiles, LANES)

    dims = (shards, own, tiles)
    theirs = send(local, 1)
    half = shaped((shards // 2 * size, LANES), f32)
    blocks = local.reshape(rows // sub * tiles, sub, 1, LANES)
    flat = [a.reshape(size, 1, LANES) for a in (master, moment, second)]
    picked = shaped((half.shape[0], 1, LANES), f32)
    *picks, state = (a.reshape(-1, LANES) for a in call(
        functools.partial(front_kernel, dims), (picked, picked, picked, shaped((3 * size, 1, LANES), f32)),
        *(pltpu.with_memory_space_constraint(a, pltpu.HBM) for a in (blocks, *flat)), hbm=True,
        scratch=[pltpu.SemaphoreType.DMA((3 + 3 * (half.shape[0] // tiles),))]))
    theirs_state = send(state, shards, 2)
    to_cross, to_near, to_level, keep = call(functools.partial(sum_kernel, dims), (half,) * 4, theirs, *picks)

    for bit in reversed(far):
        low = (shard & bit) == 0
        held = jnp.stack([keep, to_level, to_near]).reshape(3, 2, 2, -1, LANES)
        mine = jnp.where(low, held[:, :, 0], held[:, :, 1])
        other = jnp.where(low, held[:, :, 1], held[:, :, 0])
        keep, to_level, to_near = (mine + send(other, bit)).reshape(3, -1, LANES)
        to_cross = to_near

    cross = send(to_cross, shards | 3)
    near, level = send(to_near, shards | 1, 3), send(to_level, 3, shards | 1)
    sums = (cross, near, level, keep)

    params = call(
        functools.partial(params_kernel, size), shaped((2 * size, LANES), jnp.bfloat16),
        step, *sums, state, theirs_state)
    row = shaped((size, LANES), f32)
    news = call(
        functools.partial(own_kernel, size), (row, row, row), step, *sums, state)

    pieces = [send(params, 2, shards), send(params, 3, shards | 1), send(params, 1), params]
    block, sub = 8 * own, min(8, 8 * own)
    params = call(
        functools.partial(order_kernel, own, tiles), shaped((block * tiles, LANES), jnp.bfloat16),
        *pieces, scratch=[pltpu.VMEM((block * tiles, LANES), f32)])
    params = params.reshape(block // sub, tiles, sub, LANES).transpose(0, 2, 1, 3).reshape(2, 4 * own, width)
    for bit in far:
        low, got = (shard & bit) == 0, send(params, bit)
        params = jnp.concatenate([jnp.where(low, params, got), jnp.where(low, got, params)], axis=1)
    return tuple(n.reshape(own, width) for n in news) + (params.reshape(rows, width),)


def solution(mesh):
    placed = (
        P(("section", "pair"), "dp", None, None),
        P(("section", "pair", "dp"), None),
        P(("section", "pair", "dp"), None),
        P(("section", "pair", "dp"), None),
        P("section"),
    )
    return jax.shard_map(
        per_device,
        mesh=mesh,
        in_specs=placed,
        out_specs=(
            P(("section", "pair", "dp"), None),
            P(("section", "pair", "dp"), None),
            P(("section", "pair", "dp"), None),
            P("section", None),
        ),
        check_vma=False,
    )
```

```python
import functools
import math

import jax
import jax.numpy as jnp
from jax import lax
from jax.experimental import pallas as pl
from jax.experimental.pallas import tpu as pltpu
from jax.sharding import PartitionSpec as P

GROUP = ("pair", "dp")
LANES = 128


def send(array, bits, core_1_bits=None):
    size = lax.axis_size(GROUP)
    flip = (bits, bits if core_1_bits is None else core_1_bits)
    return lax.ppermute(array, GROUP, [(i, i ^ flip[i & 1]) for i in range(size)])


def row_at(row, tiles, rows):
    sub = min(8, rows)
    return pl.ds((row // sub) * (tiles * sub) + row % sub, tiles, stride=sub)


def place(core, slot, other):
    pair, near = lax.axis_index("pair"), (lax.axis_index("dp") >> 1) & 1
    return pair ^ (slot * (1 - core)) ^ (other * core), near ^ (slot * core) ^ (other * (1 - core))


def my_rows(shards, own, tiles):
    core, i = lax.axis_index("dp") & 1, 0
    for slot in range(2):
        places = [(*place(c, slot, other), c) for c, other in ((core, 0), (1 - core, 0), (1 - core, 1))]
        for far in range(shards // 4):
            for o in range(own):
                yield pl.ds(i * tiles, tiles), [
                    (pair * shards + far * 4 + near * 2 + c) * own + o for pair, near, c in places
                ]
                i += 1


def front_kernel(dims, local, master, moment, second, keep_ref, level_ref, give_ref, state_ref, sems):
    size, tiles, sub = master.shape[0], dims[2], local.shape[1]
    copies = []
    for i, source in enumerate((master, moment, second)):
        copies.append((source, state_ref.at[pl.ds(i * size, size)]))
    for to, rows in my_rows(*dims):
        for row, out_ref in zip(rows, (keep_ref, level_ref, give_ref)):
            block = pl.ds((row // sub) * tiles, tiles)
            copies.append((local.at[block, row % sub], out_ref.at[to]))
    copies = [pltpu.make_async_copy(*c, sems.at[i]) for i, c in enumerate(copies)]
    for copy in copies:
        copy.start()
    for copy in copies:
        copy.wait()


def sum_kernel(dims, theirs, own_keep, own_level, own_give, cross_ref, near_ref, level_ref, keep_ref):
    tiles, rows = dims[2], 2 * dims[0] * dims[1]
    for to, (kept, level, given) in my_rows(*dims):
        keep_ref[to, :] = own_keep[to, :] + theirs[row_at(kept, tiles, rows), :]
        level_ref[to, :] = own_level[to, :] + theirs[row_at(level, tiles, rows), :]
        give = own_give[to, :] + theirs[row_at(given, tiles, rows), :]
        cross_ref[to, :] = give
        near_ref[to, :] = give


def adam(total, master, moment, second, count):
    new_moment = 0.9 * moment + 0.1 * total
    new_second = 0.95 * second + 0.05 * total * total
    first_fix = 1.0 - jnp.exp(count * jnp.log(jnp.full_like(count, 0.9)))
    second_fix = 1.0 - jnp.exp(count * jnp.log(jnp.full_like(count, 0.95)))
    update = new_moment / first_fix / (jnp.sqrt(new_second / second_fix) + 1e-08) + 0.1 * master
    return master - 0.03 * update, new_moment, new_second


def totals(size, sums):
    cross, near, level, keep = (s[...] for s in sums)
    flip = lambda rows: (rows[size:], rows[:size])
    return [
        (c + n) + (l + k)
        for c, n, l, k in zip(flip(cross), flip(near)[::-1], flip(level), flip(keep)[::-1])
    ]


def thirds(size, ref):
    return [ref[i * size:(i + 1) * size, :] for i in range(3)]


def params_kernel(size, step_ref, cross, near, level, keep, state, theirs_state, out_ref):
    count = jnp.full((1, LANES), step_ref[0], jnp.int32).astype(jnp.float32)
    mine, theirs = totals(size, (cross, near, level, keep))
    a, _, _ = adam(mine, *thirds(size, state), count)
    b, _, _ = adam(theirs, *thirds(size, theirs_state), count)
    out_ref[...] = jnp.concatenate([a, b], axis=0).astype(out_ref.dtype)


def own_kernel(size, step_ref, cross, near, level, keep, state, m_ref, v_ref, s_ref):
    count = jnp.full((1, LANES), step_ref[0], jnp.int32).astype(jnp.float32)
    mine, _ = totals(size, (cross, near, level, keep))
    m_ref[...], v_ref[...], s_ref[...] = adam(mine, *thirds(size, state), count)


def order_kernel(own, tiles, *refs):
    pieces, out_ref, scratch = refs[:4], refs[4], refs[5]
    pair, shard = lax.axis_index("pair"), lax.axis_index("dp")
    core, near = shard & 1, (shard >> 1) & 1
    sources = (
        (pair ^ (1 - core), near ^ core, core ^ 1),
        (pair ^ core, near ^ (1 - core), core),
        (pair, near, core ^ 1),
        (pair, near, core),
    )
    for ref, (p, n, c) in zip(pieces, sources):
        piece = ref[...].astype(jnp.float32)
        for slot in range(2):
            for o in range(own):
                row = ((p ^ (slot * (1 - c))) * 4 + (n ^ (slot * c)) * 2 + c) * own + o
                start = (slot * own + o) * tiles
                scratch[row_at(row, tiles, 8 * own), :] = piece[start:start + tiles]
    out_ref[...] = scratch[...].astype(out_ref.dtype)


def call(body, outs, *args, hbm=False, scratch=()):
    space = pltpu.HBM if hbm else pltpu.VMEM
    specs = [pl.BlockSpec(memory_space=pltpu.SMEM if a.dtype == jnp.int32 else space) for a in args]
    held = sum(math.prod(a.shape) * a.dtype.itemsize for a in [*args, *jax.tree.leaves(outs)])
    return pl.pallas_call(
        body,
        out_shape=outs,
        in_specs=specs,
        out_specs=jax.tree.map(lambda _: pl.BlockSpec(memory_space=pltpu.VMEM), outs),
        scratch_shapes=list(scratch),
        compiler_params=pltpu.CompilerParams(vmem_limit_bytes=4 * held + (1 << 20)),
    )(*args)


def per_device(grads, master, moment, second, step):
    rows, width = grads.shape[2], grads.shape[3]
    own, tiles = master.shape[0], width // LANES
    shards = lax.axis_size("dp")
    shard = lax.axis_index("dp")
    far = [1 << b for b in range(2, (shards - 1).bit_length())]
    size, f32 = own * tiles, jnp.float32
    shaped = jax.ShapeDtypeStruct

    master, moment, second = (a.reshape(size, LANES) for a in (master, moment, second))
    sub = min(8, rows)
    local = grads.reshape(rows // sub, sub, tiles, LANES).transpose(0, 2, 1, 3).reshape(rows * tiles, LANES)

    dims = (shards, own, tiles)
    theirs = send(local, 1)
    half = shaped((shards // 2 * size, LANES), f32)
    blocks = local.reshape(rows // sub * tiles, sub, 1, LANES)
    flat = [a.reshape(size, 1, LANES) for a in (master, moment, second)]
    picked = shaped((half.shape[0], 1, LANES), f32)
    *picks, state = (a.reshape(-1, LANES) for a in call(
        functools.partial(front_kernel, dims), (picked, picked, picked, shaped((3 * size, 1, LANES), f32)),
        *(pltpu.with_memory_space_constraint(a, pltpu.HBM) for a in (blocks, *flat)), hbm=True,
        scratch=[pltpu.SemaphoreType.DMA((3 + 3 * (half.shape[0] // tiles),))]))
    theirs_state = send(state, shards, 2)
    to_cross, to_near, to_level, keep = call(functools.partial(sum_kernel, dims), (half,) * 4, theirs, *picks)

    for bit in reversed(far):
        low = (shard & bit) == 0
        held = jnp.stack([keep, to_level, to_near]).reshape(3, 2, 2, -1, LANES)
        mine = jnp.where(low, held[:, :, 0], held[:, :, 1])
        other = jnp.where(low, held[:, :, 1], held[:, :, 0])
        keep, to_level, to_near = (mine + send(other, bit)).reshape(3, -1, LANES)
        to_cross = to_near

    cross = send(to_cross, shards | 3)
    near, level = send(to_near, shards | 1, 3), send(to_level, 3, shards | 1)
    sums = (cross, near, level, keep)

    params = call(
        functools.partial(params_kernel, size), shaped((2 * size, LANES), jnp.bfloat16),
        step, *sums, state, theirs_state)
    row = shaped((size, LANES), f32)
    news = call(
        functools.partial(own_kernel, size), (row, row, row), step, *sums, state)

    pieces = [send(params, 3, shards | 1), send(params, 2, shards), send(params, 1), params]
    block, sub = 8 * own, min(8, 8 * own)
    params = call(
        functools.partial(order_kernel, own, tiles), shaped((block * tiles, LANES), jnp.bfloat16),
        *pieces, scratch=[pltpu.VMEM((block * tiles, LANES), f32)])
    params = params.reshape(block // sub, tiles, sub, LANES).transpose(0, 2, 1, 3).reshape(2, 4 * own, width)
    for bit in far:
        low, got = (shard & bit) == 0, send(params, bit)
        params = jnp.concatenate([jnp.where(low, params, got), jnp.where(low, got, params)], axis=1)
    return tuple(n.reshape(own, width) for n in news) + (params.reshape(rows, width),)


def solution(mesh):
    placed = (
        P(("section", "pair"), "dp", None, None),
        P(("section", "pair", "dp"), None),
        P(("section", "pair", "dp"), None),
        P(("section", "pair", "dp"), None),
        P("section"),
    )
    return jax.shard_map(
        per_device,
        mesh=mesh,
        in_specs=placed,
        out_specs=(
            P(("section", "pair", "dp"), None),
            P(("section", "pair", "dp"), None),
            P(("section", "pair", "dp"), None),
            P("section", None),
        ),
        check_vma=False,
    )
```

```python
import functools
import math

import jax
import jax.numpy as jnp
from jax import lax
from jax.experimental import pallas as pl
from jax.experimental.pallas import tpu as pltpu
from jax.sharding import PartitionSpec as P

GROUP = ("pair", "dp")
LANES = 128


def send(array, bits, core_1_bits=None):
    size = lax.axis_size(GROUP)
    flip = (bits, bits if core_1_bits is None else core_1_bits)
    return lax.ppermute(array, GROUP, [(i, i ^ flip[i & 1]) for i in range(size)])


def row_at(row, tiles, rows):
    sub = min(8, rows)
    return pl.ds((row // sub) * (tiles * sub) + row % sub, tiles, stride=sub)


def place(slot, other):
    pair, shard = lax.axis_index("pair"), lax.axis_index("dp")
    core, near = shard & 1, (shard >> 1) & 1
    return pair ^ (slot * (1 - core)) ^ (other * core), near ^ (slot * core) ^ (other * (1 - core))


def my_rows(shards, own, tiles):
    core, i = lax.axis_index("dp") & 1, 0
    for slot in range(2):
        kept, given = place(slot, 0), place(slot, 1)
        for far in range(shards // 4):
            for o in range(own):
                yield pl.ds(i * tiles, tiles), [
                    (pair * shards + far * 4 + near * 2 + core) * own + o for pair, near in (kept, given)
                ]
                i += 1


def front_kernel(dims, local, master, moment, second, keep_ref, give_ref, state_ref, sems):
    size, tiles, sub = master.shape[0], dims[2], local.shape[1]
    copies = []
    for i, source in enumerate((master, moment, second)):
        copies.append((source, state_ref.at[pl.ds(i * size, size)]))
    for to, rows in my_rows(*dims):
        for row, out_ref in zip(rows, (keep_ref, give_ref)):
            block = pl.ds((row // sub) * tiles, tiles)
            copies.append((local.at[block, row % sub], out_ref.at[to]))
    copies = [pltpu.make_async_copy(*c, sems.at[i]) for i, c in enumerate(copies)]
    for copy in copies:
        copy.start()
    for copy in copies:
        copy.wait()


def sum_kernel(dims, theirs, own_keep, own_give, state, level_ref, cross_ref, near_ref, keep_ref):
    tiles, rows = dims[2], 2 * dims[0] * dims[1]
    for to, (kept, given) in my_rows(*dims):
        keep = own_keep[to, :] + theirs[row_at(kept, tiles, rows), :]
        keep_ref[to, :] = keep
        level_ref[to, :] = keep
        give = own_give[to, :] + theirs[row_at(given, tiles, rows), :]
        cross_ref[to, :] = give
        near_ref[to, :] = give
    level_ref[keep_ref.shape[0]:, :] = state[...]


def adam(total, master, moment, second, count):
    new_moment = 0.9 * moment + 0.1 * total
    new_second = 0.95 * second + 0.05 * total * total
    first_fix = 1.0 - jnp.exp(count * jnp.log(jnp.full_like(count, 0.9)))
    second_fix = 1.0 - jnp.exp(count * jnp.log(jnp.full_like(count, 0.95)))
    update = new_moment / first_fix / (jnp.sqrt(new_second / second_fix) + 1e-08) + 0.1 * master
    return master - 0.03 * update, new_moment, new_second


def totals(size, sums):
    level, cross, near, keep = (s[:2 * size] for s in sums)
    flip = lambda rows: (rows[size:], rows[:size])
    return [
        (c + n) + (l + k)
        for c, n, l, k in zip(flip(cross), flip(near)[::-1], flip(level), flip(keep)[::-1])
    ]


def thirds(size, ref):
    return [ref[i * size:(i + 1) * size, :] for i in range(3)]


def params_kernel(size, step_ref, level, cross, near, keep, state, out_ref):
    count = jnp.full((1, LANES), step_ref[0], jnp.int32).astype(jnp.float32)
    mine, theirs = totals(size, (level, cross, near, keep))
    a, _, _ = adam(mine, *thirds(size, state), count)
    b, _, _ = adam(theirs, *thirds(size, level.at[pl.ds(2 * size, 3 * size)]), count)
    out_ref[...] = jnp.concatenate([a, b], axis=0).astype(out_ref.dtype)


def own_kernel(size, step_ref, level, cross, near, keep, state, m_ref, v_ref, s_ref):
    count = jnp.full((1, LANES), step_ref[0], jnp.int32).astype(jnp.float32)
    mine, _ = totals(size, (level, cross, near, keep))
    m_ref[...], v_ref[...], s_ref[...] = adam(mine, *thirds(size, state), count)


def order_kernel(own, tiles, *refs):
    pieces, out_ref, scratch = refs[:4], refs[4], refs[5]
    pair, shard = lax.axis_index("pair"), lax.axis_index("dp")
    core, near = shard & 1, (shard >> 1) & 1
    sources = (
        (pair ^ (1 - core), near ^ core, core ^ 1),
        (pair ^ core, near ^ (1 - core), core),
        (pair, near, core ^ 1),
        (pair, near, core),
    )
    for ref, (p, n, c) in zip(pieces, sources):
        piece = ref[...].astype(jnp.float32)
        for slot in range(2):
            for o in range(own):
                row = ((p ^ (slot * (1 - c))) * 4 + (n ^ (slot * c)) * 2 + c) * own + o
                start = (slot * own + o) * tiles
                scratch[row_at(row, tiles, 8 * own), :] = piece[start:start + tiles]
    out_ref[...] = scratch[...].astype(out_ref.dtype)


def call(body, outs, *args, hbm=False, scratch=()):
    space = pltpu.HBM if hbm else pltpu.VMEM
    specs = [pl.BlockSpec(memory_space=pltpu.SMEM if a.dtype == jnp.int32 else space) for a in args]
    held = sum(math.prod(a.shape) * a.dtype.itemsize for a in [*args, *jax.tree.leaves(outs)])
    return pl.pallas_call(
        body,
        out_shape=outs,
        in_specs=specs,
        out_specs=jax.tree.map(lambda _: pl.BlockSpec(memory_space=pltpu.VMEM), outs),
        scratch_shapes=list(scratch),
        compiler_params=pltpu.CompilerParams(vmem_limit_bytes=4 * held + (1 << 20)),
    )(*args)


def per_device(grads, master, moment, second, step):
    rows, width = grads.shape[2], grads.shape[3]
    own, tiles = master.shape[0], width // LANES
    shards = lax.axis_size("dp")
    shard = lax.axis_index("dp")
    far = [1 << b for b in range(2, (shards - 1).bit_length())]
    size, f32 = own * tiles, jnp.float32
    shaped = jax.ShapeDtypeStruct

    master, moment, second = (a.reshape(size, LANES) for a in (master, moment, second))
    sub = min(8, rows)
    local = grads.reshape(rows // sub, sub, tiles, LANES).transpose(0, 2, 1, 3).reshape(rows * tiles, LANES)

    dims = (shards, own, tiles)
    theirs = send(local, 1)
    half = shaped((shards // 2 * size, LANES), f32)
    blocks = local.reshape(rows // sub * tiles, sub, 1, LANES)
    flat = [a.reshape(size, 1, LANES) for a in (master, moment, second)]
    picked = shaped((half.shape[0], 1, LANES), f32)
    keep, give, state = (a.reshape(-1, LANES) for a in call(
        functools.partial(front_kernel, dims), (picked, picked, shaped((3 * size, 1, LANES), f32)),
        *(pltpu.with_memory_space_constraint(a, pltpu.HBM) for a in (blocks, *flat)), hbm=True,
        scratch=[pltpu.SemaphoreType.DMA((3 + 2 * (half.shape[0] // tiles),))]))
    joined = shaped((half.shape[0] + 3 * size, LANES), f32)
    to_level, to_cross, to_near, keep = call(
        functools.partial(sum_kernel, dims), (joined, half, half, half), theirs, keep, give, state)

    for bit in reversed(far):
        low = (shard & bit) == 0
        held = jnp.stack([keep, to_near]).reshape(2, 2, 2, -1, LANES)
        mine = jnp.where(low, held[:, :, 0], held[:, :, 1])
        other = jnp.where(low, held[:, :, 1], held[:, :, 0])
        keep, to_near = (mine + send(other, bit)).reshape(2, -1, LANES)
        to_cross, to_level = to_near, jnp.concatenate([keep, state], axis=0)

    level, cross, near = send(to_level, shards, 2), send(to_cross, shards | 2), send(to_near, 2, shards)
    sums = (level, cross, near, keep)

    params = call(
        functools.partial(params_kernel, size), shaped((2 * size, LANES), jnp.bfloat16),
        step, *sums, state)
    row = shaped((size, LANES), f32)
    news = call(
        functools.partial(own_kernel, size), (row, row, row), step, *sums, state)

    pieces = [send(params, 3, shards | 1), send(params, 2, shards), send(params, 1), params]
    block, sub = 8 * own, min(8, 8 * own)
    params = call(
        functools.partial(order_kernel, own, tiles), shaped((block * tiles, LANES), jnp.bfloat16),
        *pieces, scratch=[pltpu.VMEM((block * tiles, LANES), f32)])
    params = params.reshape(block // sub, tiles, sub, LANES).transpose(0, 2, 1, 3).reshape(2, 4 * own, width)
    for bit in far:
        low, got = (shard & bit) == 0, send(params, bit)
        params = jnp.concatenate([jnp.where(low, params, got), jnp.where(low, got, params)], axis=1)
    return tuple(n.reshape(own, width) for n in news) + (params.reshape(rows, width),)


def solution(mesh):
    placed = (
        P(("section", "pair"), "dp", None, None),
        P(("section", "pair", "dp"), None),
        P(("section", "pair", "dp"), None),
        P(("section", "pair", "dp"), None),
        P("section"),
    )
    return jax.shard_map(
        per_device,
        mesh=mesh,
        in_specs=placed,
        out_specs=(
            P(("section", "pair", "dp"), None),
            P(("section", "pair", "dp"), None),
            P(("section", "pair", "dp"), None),
            P("section", None),
        ),
        check_vma=False,
    )
```

```python
import functools
import math

import jax
import jax.numpy as jnp
from jax import lax
from jax.experimental import pallas as pl
from jax.experimental.pallas import tpu as pltpu
from jax.sharding import PartitionSpec as P

GROUP = ("pair", "dp")
LANES = 128
CHIPS = (1, 1), (0, 1), (1, 0), (0, 0)


BOTH, CORE_0, CORE_1 = (0, 1), (0,), (1,)


def send(array, bits, cores=BOTH):
    size = lax.axis_size(GROUP)
    return lax.ppermute(array, GROUP, [(i, i ^ bits) for i in range(size) if i & 1 in cores])


def row_at(row, tiles, rows):
    sub = min(8, rows)
    return pl.ds((row // sub) * (tiles * sub) + row % sub, tiles, stride=sub)


def front_kernel(local, master, moment, second, mine_ref, state_ref, sems):
    size = master.shape[0]
    copies = [pltpu.make_async_copy(local, mine_ref, sems.at[3])]
    for i, source in enumerate((master, moment, second)):
        to = state_ref.at[pl.ds(i * size, size), :]
        copies.append(pltpu.make_async_copy(source, to, sems.at[i]))
    for copy in copies:
        copy.start()
    for copy in copies:
        copy.wait()


def sum_kernel(shards, own, tiles, mine, theirs, *out_refs):
    pair, near = lax.axis_index("pair"), (lax.axis_index("dp") >> 1) & 1
    i, rows = 0, 2 * shards * own
    for core in range(2):
        for far in range(shards // 4):
            for o in range(own):
                to = pl.ds(i * tiles, tiles)
                for chip, out_ref in zip(CHIPS, out_refs):
                    p, n = pair ^ chip[0], near ^ chip[1]
                    at = row_at((p * shards + far * 4 + n * 2 + core) * own + o, tiles, rows)
                    out_ref[to, :] = mine[at, :] + theirs[at, :]
                i += 1


def adam(total, master, moment, second, count):
    new_moment = 0.9 * moment + 0.1 * total
    new_second = 0.95 * second + 0.05 * total * total
    first_fix = 1.0 - jnp.exp(count * jnp.log(jnp.full_like(count, 0.9)))
    second_fix = 1.0 - jnp.exp(count * jnp.log(jnp.full_like(count, 0.95)))
    update = new_moment / first_fix / (jnp.sqrt(new_second / second_fix) + 1e-08) + 0.1 * master
    return master - 0.03 * update, new_moment, new_second


def thirds(size, ref):
    return [ref[i * size:(i + 1) * size, :] for i in range(3)]


def params_kernel(size, step_ref, cross, near, level, keep, state, theirs_state, out_ref, theirs_ref, mine_ref):
    count = jnp.full((1, LANES), step_ref[0], jnp.int32).astype(jnp.float32)
    total = (keep[...] + level[...]) + (near[...] + cross[...])
    a, _, _ = adam(total[:size], *thirds(size, theirs_state), count)
    b, _, _ = adam(total[size:], *thirds(size, state), count)
    out_ref[...] = jnp.concatenate([a, b], axis=0).astype(out_ref.dtype)
    theirs_ref[...] = total[:size]
    mine_ref[...] = total[size:]


def own_kernel(size, step_ref, mine, given, state, m_ref, v_ref, s_ref):
    count = jnp.full((1, LANES), step_ref[0], jnp.int32).astype(jnp.float32)
    core = lax.axis_index("dp") & 1
    total = jnp.where(core == 1, mine[...], given[...])
    m_ref[...], v_ref[...], s_ref[...] = adam(total, *thirds(size, state), count)


def order_kernel(own, tiles, *refs):
    pieces, passed, out_ref, scratch = refs[:4], refs[4:8], refs[8], refs[9]
    pair, shard = lax.axis_index("pair"), lax.axis_index("dp")
    core, near = shard & 1, (shard >> 1) & 1
    for piece, other, chip in zip(pieces, passed, CHIPS):
        values = jnp.where(core == 1, piece[...].astype(jnp.float32), other[...].astype(jnp.float32))
        for c in range(2):
            for o in range(own):
                row = ((pair ^ chip[0]) * 4 + (near ^ chip[1]) * 2 + c) * own + o
                start = (c * own + o) * tiles
                scratch[row_at(row, tiles, 8 * own), :] = values[start:start + tiles]
    out_ref[...] = scratch[...].astype(out_ref.dtype)


def call(body, outs, *args, hbm=False, scratch=()):
    space = pltpu.HBM if hbm else pltpu.VMEM
    specs = [pl.BlockSpec(memory_space=pltpu.SMEM if a.dtype == jnp.int32 else space) for a in args]
    held = sum(math.prod(a.shape) * a.dtype.itemsize for a in [*args, *jax.tree.leaves(outs)])
    return pl.pallas_call(
        body,
        out_shape=outs,
        in_specs=specs,
        out_specs=jax.tree.map(lambda _: pl.BlockSpec(memory_space=pltpu.VMEM), outs),
        scratch_shapes=list(scratch),
        compiler_params=pltpu.CompilerParams(vmem_limit_bytes=4 * held + (1 << 20)),
    )(*args)


def per_device(grads, master, moment, second, step):
    rows, width = grads.shape[2], grads.shape[3]
    own, tiles = master.shape[0], width // LANES
    shards = lax.axis_size("dp")
    shard = lax.axis_index("dp")
    far = [1 << b for b in range(2, (shards - 1).bit_length())]
    size, f32 = own * tiles, jnp.float32
    shaped = jax.ShapeDtypeStruct

    master, moment, second = (a.reshape(size, LANES) for a in (master, moment, second))
    sub = min(8, rows)
    local = grads.reshape(rows // sub, sub, tiles, LANES).transpose(0, 2, 1, 3).reshape(rows * tiles, LANES)

    theirs = send(local, 1, CORE_0)
    mine, state = call(
        front_kernel, (shaped(local.shape, f32), shaped((3 * size, LANES), f32)),
        *(pltpu.with_memory_space_constraint(a, pltpu.HBM) for a in (local, master, moment, second)), hbm=True,
        scratch=[pltpu.SemaphoreType.DMA((4,))])
    theirs_state = send(state, 1, CORE_0)
    half = shaped((shards // 2 * size, LANES), f32)
    sums = call(functools.partial(sum_kernel, shards, own, tiles), (half,) * 4, mine, theirs)

    for bit in reversed(far):
        low = (shard & bit) == 0
        held = jnp.stack(sums).reshape(4, 2, 2, -1, LANES)
        stay = jnp.where(low, held[:, :, 0], held[:, :, 1])
        other = jnp.where(low, held[:, :, 1], held[:, :, 0])
        sums = tuple((stay + send(other, bit, CORE_1)).reshape(4, -1, LANES))

    across = [p * shards + n * 2 for p, n in CHIPS[:3]]
    sums = [send(a, bits, CORE_1) for a, bits in zip(sums, across)] + [sums[3]]
    row = shaped((size, LANES), f32)
    params, theirs_total, mine_total = call(
        functools.partial(params_kernel, size), (shaped((2 * size, LANES), jnp.bfloat16), row, row),
        step, *sums, state, theirs_state)
    pieces = [send(params, bits, CORE_1) for bits in across] + [params]
    given = send(theirs_total, 1, CORE_1)
    news = call(functools.partial(own_kernel, size), (row, row, row), step, mine_total, given, state)

    pieces += [send(p, 1, CORE_1) for p in pieces]
    block, sub = 8 * own, min(8, 8 * own)
    params = call(
        functools.partial(order_kernel, own, tiles), shaped((block * tiles, LANES), jnp.bfloat16),
        *pieces, scratch=[pltpu.VMEM((block * tiles, LANES), f32)])
    params = params.reshape(block // sub, tiles, sub, LANES).transpose(0, 2, 1, 3).reshape(2, 4 * own, width)
    for bit in far:
        low, got = (shard & bit) == 0, send(params, bit)
        params = jnp.concatenate([jnp.where(low, params, got), jnp.where(low, got, params)], axis=1)
    return tuple(n.reshape(own, width) for n in news) + (params.reshape(rows, width),)


def solution(mesh):
    placed = (
        P(("section", "pair"), "dp", None, None),
        P(("section", "pair", "dp"), None),
        P(("section", "pair", "dp"), None),
        P(("section", "pair", "dp"), None),
        P("section"),
    )
    return jax.shard_map(
        per_device,
        mesh=mesh,
        in_specs=placed,
        out_specs=(
            P(("section", "pair", "dp"), None),
            P(("section", "pair", "dp"), None),
            P(("section", "pair", "dp"), None),
            P("section", None),
        ),
        check_vma=False,
    )
```

```python
import functools
import math

import jax
import jax.numpy as jnp
from jax import lax
from jax.experimental import pallas as pl
from jax.experimental.pallas import tpu as pltpu
from jax.sharding import PartitionSpec as P

GROUP = ("pair", "dp")
LANES = 128
CHIPS = (1, 1), (0, 1), (1, 0), (0, 0)


def swap(array, bits, chips=False):
    size = lax.axis_size(GROUP)
    return lax.ppermute(array, GROUP, [(i, i if chips and i & 1 == 0 else i ^ bits) for i in range(size)])


def row_at(row, tiles, rows):
    sub = min(8, rows)
    return pl.ds((row // sub) * (tiles * sub) + row % sub, tiles, stride=sub)


def front_kernel(local, master, moment, second, mine_ref, state_ref, sems):
    size = master.shape[0]
    copies = [pltpu.make_async_copy(local, mine_ref, sems.at[3])]
    for i, source in enumerate((master, moment, second)):
        to = state_ref.at[pl.ds(i * size, size), :]
        copies.append(pltpu.make_async_copy(source, to, sems.at[i]))
    for copy in copies:
        copy.start()
    for copy in copies:
        copy.wait()


def sum_kernel(shards, own, tiles, mine, theirs, *out_refs):
    pair, near = lax.axis_index("pair"), (lax.axis_index("dp") >> 1) & 1
    i, rows = 0, 2 * shards * own
    for core in range(2):
        for far in range(shards // 4):
            for o in range(own):
                to = pl.ds(i * tiles, tiles)
                for chip, out_ref in zip(CHIPS, out_refs):
                    p, n = pair ^ chip[0], near ^ chip[1]
                    at = row_at((p * shards + far * 4 + n * 2 + core) * own + o, tiles, rows)
                    out_ref[to, :] = mine[at, :] + theirs[at, :]
                i += 1


def adam(total, master, moment, second, count):
    new_moment = 0.9 * moment + 0.1 * total
    new_second = 0.95 * second + 0.05 * total * total
    first_fix = 1.0 - jnp.exp(count * jnp.log(jnp.full_like(count, 0.9)))
    second_fix = 1.0 - jnp.exp(count * jnp.log(jnp.full_like(count, 0.95)))
    update = new_moment / first_fix / (jnp.sqrt(new_second / second_fix) + 1e-08) + 0.1 * master
    return master - 0.03 * update, new_moment, new_second


def thirds(size, ref):
    return [ref[i * size:(i + 1) * size, :] for i in range(3)]


def params_kernel(size, step_ref, cross, near, level, keep, state, theirs_state, out_ref, theirs_ref, mine_ref):
    count = jnp.full((1, LANES), step_ref[0], jnp.int32).astype(jnp.float32)
    total = (keep[...] + level[...]) + (near[...] + cross[...])
    a, _, _ = adam(total[:size], *thirds(size, theirs_state), count)
    b, _, _ = adam(total[size:], *thirds(size, state), count)
    out_ref[...] = jnp.concatenate([a, b], axis=0).astype(out_ref.dtype)
    theirs_ref[...] = total[:size]
    mine_ref[...] = total[size:]


def own_kernel(size, step_ref, mine, given, state, m_ref, v_ref, s_ref):
    count = jnp.full((1, LANES), step_ref[0], jnp.int32).astype(jnp.float32)
    core = lax.axis_index("dp") & 1
    total = jnp.where(core == 1, mine[...], given[...])
    m_ref[...], v_ref[...], s_ref[...] = adam(total, *thirds(size, state), count)


def order_kernel(own, tiles, *refs):
    pieces, passed, out_ref, scratch = refs[:4], refs[4:8], refs[8], refs[9]
    pair, shard = lax.axis_index("pair"), lax.axis_index("dp")
    core, near = shard & 1, (shard >> 1) & 1
    for piece, other, chip in zip(pieces, passed, CHIPS):
        values = jnp.where(core == 1, piece[...].astype(jnp.float32), other[...].astype(jnp.float32))
        for c in range(2):
            for o in range(own):
                row = ((pair ^ chip[0]) * 4 + (near ^ chip[1]) * 2 + c) * own + o
                start = (c * own + o) * tiles
                scratch[row_at(row, tiles, 8 * own), :] = values[start:start + tiles]
    out_ref[...] = scratch[...].astype(out_ref.dtype)


def call(body, outs, *args, hbm=False, scratch=()):
    space = pltpu.HBM if hbm else pltpu.VMEM
    specs = [pl.BlockSpec(memory_space=pltpu.SMEM if a.dtype == jnp.int32 else space) for a in args]
    held = sum(math.prod(a.shape) * a.dtype.itemsize for a in [*args, *jax.tree.leaves(outs)])
    return pl.pallas_call(
        body,
        out_shape=outs,
        in_specs=specs,
        out_specs=jax.tree.map(lambda _: pl.BlockSpec(memory_space=pltpu.VMEM), outs),
        scratch_shapes=list(scratch),
        compiler_params=pltpu.CompilerParams(vmem_limit_bytes=4 * held + (1 << 20)),
    )(*args)


def per_device(grads, master, moment, second, step):
    rows, width = grads.shape[2], grads.shape[3]
    own, tiles = master.shape[0], width // LANES
    shards = lax.axis_size("dp")
    shard = lax.axis_index("dp")
    far = [1 << b for b in range(2, (shards - 1).bit_length())]
    size, f32 = own * tiles, jnp.float32
    shaped = jax.ShapeDtypeStruct

    master, moment, second = (a.reshape(size, LANES) for a in (master, moment, second))
    sub = min(8, rows)
    local = grads.reshape(rows // sub, sub, tiles, LANES).transpose(0, 2, 1, 3).reshape(rows * tiles, LANES)

    theirs = swap(local, 1)
    mine, state = call(
        front_kernel, (shaped(local.shape, f32), shaped((3 * size, LANES), f32)),
        *(pltpu.with_memory_space_constraint(a, pltpu.HBM) for a in (local, master, moment, second)), hbm=True,
        scratch=[pltpu.SemaphoreType.DMA((4,))])
    theirs_state = swap(state, 1)
    half = shaped((shards // 2 * size, LANES), f32)
    sums = call(functools.partial(sum_kernel, shards, own, tiles), (half,) * 4, mine, theirs)

    for bit in reversed(far):
        low = (shard & bit) == 0
        held = jnp.stack(sums).reshape(4, 2, 2, -1, LANES)
        stay = jnp.where(low, held[:, :, 0], held[:, :, 1])
        other = jnp.where(low, held[:, :, 1], held[:, :, 0])
        sums = tuple((stay + swap(other, bit, True)).reshape(4, -1, LANES))

    across = [p * shards + n * 2 for p, n in CHIPS[:3]]
    sums = [swap(a, bits, True) for a, bits in zip(sums, across)] + [sums[3]]
    row = shaped((size, LANES), f32)
    params, theirs_total, mine_total = call(
        functools.partial(params_kernel, size), (shaped((2 * size, LANES), jnp.bfloat16), row, row),
        step, *sums, state, theirs_state)
    pieces = [swap(params, bits, True) for bits in across] + [params]
    given = swap(theirs_total, 1)
    news = call(functools.partial(own_kernel, size), (row, row, row), step, mine_total, given, state)

    pieces += [swap(p, 1) for p in pieces]
    block, sub = 8 * own, min(8, 8 * own)
    params = call(
        functools.partial(order_kernel, own, tiles), shaped((block * tiles, LANES), jnp.bfloat16),
        *pieces, scratch=[pltpu.VMEM((block * tiles, LANES), f32)])
    params = params.reshape(block // sub, tiles, sub, LANES).transpose(0, 2, 1, 3).reshape(2, 4 * own, width)
    for bit in far:
        low, got = (shard & bit) == 0, swap(params, bit)
        params = jnp.concatenate([jnp.where(low, params, got), jnp.where(low, got, params)], axis=1)
    return tuple(n.reshape(own, width) for n in news) + (params.reshape(rows, width),)


def solution(mesh):
    placed = (
        P(("section", "pair"), "dp", None, None),
        P(("section", "pair", "dp"), None),
        P(("section", "pair", "dp"), None),
        P(("section", "pair", "dp"), None),
        P("section"),
    )
    return jax.shard_map(
        per_device,
        mesh=mesh,
        in_specs=placed,
        out_specs=(
            P(("section", "pair", "dp"), None),
            P(("section", "pair", "dp"), None),
            P(("section", "pair", "dp"), None),
            P("section", None),
        ),
        check_vma=False,
    )
```

```python
import functools
import math

import jax
import jax.numpy as jnp
from jax import lax
from jax.experimental import pallas as pl
from jax.experimental.pallas import tpu as pltpu
from jax.sharding import PartitionSpec as P

GROUP = ("pair", "dp")
LANES = 128


def send(array, bits, core_1_bits=None):
    size = lax.axis_size(GROUP)
    flip = (bits, bits if core_1_bits is None else core_1_bits)
    return lax.ppermute(array, GROUP, [(i, i ^ flip[i & 1]) for i in range(size)])


def row_at(row, tiles, rows):
    sub = min(8, rows)
    return pl.ds((row // sub) * (tiles * sub) + row % sub, tiles, stride=sub)


def place(slot, other):
    pair, shard = lax.axis_index("pair"), lax.axis_index("dp")
    core, near = shard & 1, (shard >> 1) & 1
    return pair ^ (slot * (1 - core)) ^ (other * core), near ^ (slot * core) ^ (other * (1 - core))


def my_rows(shards, own, tiles):
    core, i = lax.axis_index("dp") & 1, 0
    for slot in range(2):
        kept, given = place(slot, 0), place(slot, 1)
        for far in range(shards // 4):
            for o in range(own):
                yield pl.ds(i * tiles, tiles), [
                    (pair * shards + far * 4 + near * 2 + core) * own + o for pair, near in (kept, given)
                ]
                i += 1


def front_kernel(dims, local, master, moment, second, keep_ref, give_ref, state_ref, sems):
    size, tiles, sub = master.shape[0], dims[2], local.shape[1]
    copies = []
    for i, source in enumerate((master, moment, second)):
        copies.append((source, state_ref.at[pl.ds(i * size, size)]))
    for to, rows in my_rows(*dims):
        for row, out_ref in zip(rows, (keep_ref, give_ref)):
            block = pl.ds((row // sub) * tiles, tiles)
            copies.append((local.at[block, row % sub], out_ref.at[to]))
    copies = [pltpu.make_async_copy(*c, sems.at[i]) for i, c in enumerate(copies)]
    for copy in copies:
        copy.start()
    for copy in copies:
        copy.wait()


def sum_kernel(dims, theirs, own_keep, own_give, cross_ref, near_ref, level_ref, keep_ref):
    tiles, rows = dims[2], 2 * dims[0] * dims[1]
    for to, (kept, given) in my_rows(*dims):
        keep = own_keep[to, :] + theirs[row_at(kept, tiles, rows), :]
        keep_ref[to, :] = keep
        level_ref[to, :] = keep
        give = own_give[to, :] + theirs[row_at(given, tiles, rows), :]
        cross_ref[to, :] = give
        near_ref[to, :] = give


def adam(total, master, moment, second, count):
    new_moment = 0.9 * moment + 0.1 * total
    new_second = 0.95 * second + 0.05 * total * total
    first_fix = 1.0 - jnp.exp(count * jnp.log(jnp.full_like(count, 0.9)))
    second_fix = 1.0 - jnp.exp(count * jnp.log(jnp.full_like(count, 0.95)))
    update = new_moment / first_fix / (jnp.sqrt(new_second / second_fix) + 1e-08) + 0.1 * master
    return master - 0.03 * update, new_moment, new_second


def totals(size, sums):
    level, cross, near, keep = (s[...] for s in sums)
    flip = lambda rows: (rows[size:], rows[:size])
    return [
        (c + n) + (l + k)
        for c, n, l, k in zip(flip(cross), flip(near)[::-1], flip(level), flip(keep)[::-1])
    ]


def thirds(size, ref):
    return [ref[i * size:(i + 1) * size, :] for i in range(3)]


def params_kernel(size, step_ref, level, cross, near, keep, state, theirs_state, out_ref):
    count = jnp.full((1, LANES), step_ref[0], jnp.int32).astype(jnp.float32)
    mine, theirs = totals(size, (level, cross, near, keep))
    a, _, _ = adam(mine, *thirds(size, state), count)
    b, _, _ = adam(theirs, *thirds(size, theirs_state), count)
    out_ref[...] = jnp.concatenate([a, b], axis=0).astype(out_ref.dtype)


def own_kernel(size, step_ref, level, cross, near, keep, state, m_ref, v_ref, s_ref):
    count = jnp.full((1, LANES), step_ref[0], jnp.int32).astype(jnp.float32)
    mine, _ = totals(size, (level, cross, near, keep))
    m_ref[...], v_ref[...], s_ref[...] = adam(mine, *thirds(size, state), count)


def order_kernel(own, tiles, *refs):
    pieces, out_ref, scratch = refs[:4], refs[4], refs[5]
    pair, shard = lax.axis_index("pair"), lax.axis_index("dp")
    core, near = shard & 1, (shard >> 1) & 1
    sources = (
        (pair ^ (1 - core), near ^ core, core ^ 1),
        (pair ^ core, near ^ (1 - core), core),
        (pair, near, core ^ 1),
        (pair, near, core),
    )
    for ref, (p, n, c) in zip(pieces, sources):
        piece = ref[...].astype(jnp.float32)
        for slot in range(2):
            for o in range(own):
                row = ((p ^ (slot * (1 - c))) * 4 + (n ^ (slot * c)) * 2 + c) * own + o
                start = (slot * own + o) * tiles
                scratch[row_at(row, tiles, 8 * own), :] = piece[start:start + tiles]
    out_ref[...] = scratch[...].astype(out_ref.dtype)


def call(body, outs, *args, hbm=False, scratch=()):
    space = pltpu.HBM if hbm else pltpu.VMEM
    specs = [pl.BlockSpec(memory_space=pltpu.SMEM if a.dtype == jnp.int32 else space) for a in args]
    held = sum(math.prod(a.shape) * a.dtype.itemsize for a in [*args, *jax.tree.leaves(outs)])
    return pl.pallas_call(
        body,
        out_shape=outs,
        in_specs=specs,
        out_specs=jax.tree.map(lambda _: pl.BlockSpec(memory_space=pltpu.VMEM), outs),
        scratch_shapes=list(scratch),
        compiler_params=pltpu.CompilerParams(vmem_limit_bytes=4 * held + (1 << 20)),
    )(*args)


def per_device(grads, master, moment, second, step):
    rows, width = grads.shape[2], grads.shape[3]
    own, tiles = master.shape[0], width // LANES
    shards = lax.axis_size("dp")
    shard = lax.axis_index("dp")
    far = [1 << b for b in range(2, (shards - 1).bit_length())]
    size, f32 = own * tiles, jnp.float32
    shaped = jax.ShapeDtypeStruct

    master, moment, second = (a.reshape(size, LANES) for a in (master, moment, second))
    sub = min(8, rows)
    local = grads.reshape(rows // sub, sub, tiles, LANES).transpose(0, 2, 1, 3).reshape(rows * tiles, LANES)

    dims = (shards, own, tiles)
    theirs = send(local, 1)
    half = shaped((shards // 2 * size, LANES), f32)
    blocks = local.reshape(rows // sub * tiles, sub, 1, LANES)
    flat = [a.reshape(size, 1, LANES) for a in (master, moment, second)]
    picked = shaped((half.shape[0], 1, LANES), f32)
    keep, give, state = (a.reshape(-1, LANES) for a in call(
        functools.partial(front_kernel, dims), (picked, picked, shaped((3 * size, 1, LANES), f32)),
        *(pltpu.with_memory_space_constraint(a, pltpu.HBM) for a in (blocks, *flat)), hbm=True,
        scratch=[pltpu.SemaphoreType.DMA((3 + 2 * (half.shape[0] // tiles),))]))
    theirs_state = send(state, shards, 2)
    to_cross, to_near, to_level, keep = call(functools.partial(sum_kernel, dims), (half, half, half, half), theirs, keep, give)

    for bit in reversed(far):
        low = (shard & bit) == 0
        held = jnp.stack([keep, to_near]).reshape(2, 2, 2, -1, LANES)
        mine = jnp.where(low, held[:, :, 0], held[:, :, 1])
        other = jnp.where(low, held[:, :, 1], held[:, :, 0])
        keep, to_near = (mine + send(other, bit)).reshape(2, -1, LANES)
        to_cross, to_level = to_near, keep

    cross, near, level = send(to_cross, shards | 2), send(to_near, 2, shards), send(to_level, shards, 2)
    sums = (level, cross, near, keep)

    params = call(
        functools.partial(params_kernel, size), shaped((2 * size, LANES), jnp.bfloat16),
        step, *sums, state, theirs_state)
    row = shaped((size, LANES), f32)
    news = call(
        functools.partial(own_kernel, size), (row, row, row), step, *sums, state)

    pieces = [send(params, 3, shards | 1), send(params, 2, shards), send(params, 1), params]
    block, sub = 8 * own, min(8, 8 * own)
    params = call(
        functools.partial(order_kernel, own, tiles), shaped((block * tiles, LANES), jnp.bfloat16),
        *pieces, scratch=[pltpu.VMEM((block * tiles, LANES), f32)])
    params = params.reshape(block // sub, tiles, sub, LANES).transpose(0, 2, 1, 3).reshape(2, 4 * own, width)
    for bit in far:
        low, got = (shard & bit) == 0, send(params, bit)
        params = jnp.concatenate([jnp.where(low, params, got), jnp.where(low, got, params)], axis=1)
    return tuple(n.reshape(own, width) for n in news) + (params.reshape(rows, width),)


def solution(mesh):
    placed = (
        P(("section", "pair"), "dp", None, None),
        P(("section", "pair", "dp"), None),
        P(("section", "pair", "dp"), None),
        P(("section", "pair", "dp"), None),
        P("section"),
    )
    return jax.shard_map(
        per_device,
        mesh=mesh,
        in_specs=placed,
        out_specs=(
            P(("section", "pair", "dp"), None),
            P(("section", "pair", "dp"), None),
            P(("section", "pair", "dp"), None),
            P("section", None),
        ),
        check_vma=False,
    )
```

```python
import functools
import math

import jax
import jax.numpy as jnp
from jax import lax
from jax.experimental import pallas as pl
from jax.experimental.pallas import tpu as pltpu
from jax.sharding import PartitionSpec as P

GROUP = ("pair", "dp")
LANES = 128
CHIPS = (1, 1), (0, 1), (1, 0), (0, 0)


def swap(array, bits):
    size = lax.axis_size(GROUP)
    return lax.ppermute(array, GROUP, [(i, i ^ bits) for i in range(size)])


def row_at(row, tiles, rows):
    sub = min(8, rows)
    return pl.ds((row // sub) * (tiles * sub) + row % sub, tiles, stride=sub)


def front_kernel(local, master, moment, second, mine_ref, state_ref, sems):
    size = master.shape[0]
    copies = [pltpu.make_async_copy(local, mine_ref, sems.at[3])]
    for i, source in enumerate((master, moment, second)):
        to = state_ref.at[pl.ds(i * size, size), :]
        copies.append(pltpu.make_async_copy(source, to, sems.at[i]))
    for copy in copies:
        copy.start()
    for copy in copies:
        copy.wait()


def sum_kernel(shards, own, tiles, mine, theirs, *out_refs):
    pair, near = lax.axis_index("pair"), (lax.axis_index("dp") >> 1) & 1
    i, rows = 0, 2 * shards * own
    for core in range(2):
        for far in range(shards // 4):
            for o in range(own):
                to = pl.ds(i * tiles, tiles)
                for chip, out_ref in zip(CHIPS, out_refs):
                    p, n = pair ^ chip[0], near ^ chip[1]
                    at = row_at((p * shards + far * 4 + n * 2 + core) * own + o, tiles, rows)
                    out_ref[to, :] = mine[at, :] + theirs[at, :]
                i += 1


def adam(total, master, moment, second, count):
    new_moment = 0.9 * moment + 0.1 * total
    new_second = 0.95 * second + 0.05 * total * total
    first_fix = 1.0 - jnp.exp(count * jnp.log(jnp.full_like(count, 0.9)))
    second_fix = 1.0 - jnp.exp(count * jnp.log(jnp.full_like(count, 0.95)))
    update = new_moment / first_fix / (jnp.sqrt(new_second / second_fix) + 1e-08) + 0.1 * master
    return master - 0.03 * update, new_moment, new_second


def thirds(size, ref):
    return [ref[i * size:(i + 1) * size, :] for i in range(3)]


def totals(sums):
    cross, near, level, keep = (s[...] for s in sums)
    return (keep + level) + (near + cross)


def params_kernel(size, step_ref, cross, near, level, keep, state, theirs_state, out_ref):
    count = jnp.full((1, LANES), step_ref[0], jnp.int32).astype(jnp.float32)
    total = totals((cross, near, level, keep))
    first = lax.axis_index("dp") & 1 == 0
    mine, theirs = thirds(size, state), thirds(size, theirs_state)
    low = [jnp.where(first, m, t) for m, t in zip(mine, theirs)]
    high = [jnp.where(first, t, m) for m, t in zip(mine, theirs)]
    a, _, _ = adam(total[:size], *low, count)
    b, _, _ = adam(total[size:], *high, count)
    out_ref[...] = jnp.concatenate([a, b], axis=0).astype(out_ref.dtype)


def own_kernel(size, step_ref, cross, near, level, keep, state, m_ref, v_ref, s_ref):
    count = jnp.full((1, LANES), step_ref[0], jnp.int32).astype(jnp.float32)
    total = totals((cross, near, level, keep))
    mine = jnp.where(lax.axis_index("dp") & 1 == 0, total[:size], total[size:])
    m_ref[...], v_ref[...], s_ref[...] = adam(mine, *thirds(size, state), count)


def order_kernel(own, tiles, *refs):
    pieces, out_ref, scratch = refs[:4], refs[4], refs[5]
    pair, near = lax.axis_index("pair"), (lax.axis_index("dp") >> 1) & 1
    for piece, chip in zip(pieces, CHIPS):
        values = piece[...].astype(jnp.float32)
        for c in range(2):
            for o in range(own):
                row = ((pair ^ chip[0]) * 4 + (near ^ chip[1]) * 2 + c) * own + o
                start = (c * own + o) * tiles
                scratch[row_at(row, tiles, 8 * own), :] = values[start:start + tiles]
    out_ref[...] = scratch[...].astype(out_ref.dtype)


def call(body, outs, *args, hbm=False, scratch=()):
    space = pltpu.HBM if hbm else pltpu.VMEM
    specs = [pl.BlockSpec(memory_space=pltpu.SMEM if a.dtype == jnp.int32 else space) for a in args]
    held = sum(math.prod(a.shape) * a.dtype.itemsize for a in [*args, *jax.tree.leaves(outs)])
    return pl.pallas_call(
        body,
        out_shape=outs,
        in_specs=specs,
        out_specs=jax.tree.map(lambda _: pl.BlockSpec(memory_space=pltpu.VMEM), outs),
        scratch_shapes=list(scratch),
        compiler_params=pltpu.CompilerParams(vmem_limit_bytes=4 * held + (1 << 20)),
    )(*args)


def per_device(grads, master, moment, second, step):
    rows, width = grads.shape[2], grads.shape[3]
    own, tiles = master.shape[0], width // LANES
    shards = lax.axis_size("dp")
    shard = lax.axis_index("dp")
    far = [1 << b for b in range(2, (shards - 1).bit_length())]
    size, f32 = own * tiles, jnp.float32
    shaped = jax.ShapeDtypeStruct

    master, moment, second = (a.reshape(size, LANES) for a in (master, moment, second))
    sub = min(8, rows)
    local = grads.reshape(rows // sub, sub, tiles, LANES).transpose(0, 2, 1, 3).reshape(rows * tiles, LANES)

    theirs = swap(local, 1)
    mine, state = call(
        front_kernel, (shaped(local.shape, f32), shaped((3 * size, LANES), f32)),
        *(pltpu.with_memory_space_constraint(a, pltpu.HBM) for a in (local, master, moment, second)), hbm=True,
        scratch=[pltpu.SemaphoreType.DMA((4,))])
    theirs_state = swap(state, 1)
    half = shaped((shards // 2 * size, LANES), f32)
    sums = call(functools.partial(sum_kernel, shards, own, tiles), (half,) * 4, mine, theirs)

    for bit in reversed(far):
        low = (shard & bit) == 0
        held = jnp.stack(sums).reshape(4, 2, 2, -1, LANES)
        stay = jnp.where(low, held[:, :, 0], held[:, :, 1])
        other = jnp.where(low, held[:, :, 1], held[:, :, 0])
        sums = tuple((stay + swap(other, bit)).reshape(4, -1, LANES))

    across = [p * shards + n * 2 + 1 for p, n in CHIPS[:3]]
    sums = [swap(a, bits) for a, bits in zip(sums, across)] + [sums[3]]
    params = call(
        functools.partial(params_kernel, size), shaped((2 * size, LANES), jnp.bfloat16),
        step, *sums, state, theirs_state)
    row = shaped((size, LANES), f32)
    news = call(functools.partial(own_kernel, size), (row, row, row), step, *sums, state)

    pieces = [swap(params, bits) for bits in across] + [params]
    block, sub = 8 * own, min(8, 8 * own)
    params = call(
        functools.partial(order_kernel, own, tiles), shaped((block * tiles, LANES), jnp.bfloat16),
        *pieces, scratch=[pltpu.VMEM((block * tiles, LANES), f32)])
    params = params.reshape(block // sub, tiles, sub, LANES).transpose(0, 2, 1, 3).reshape(2, 4 * own, width)
    for bit in far:
        low, got = (shard & bit) == 0, swap(params, bit)
        params = jnp.concatenate([jnp.where(low, params, got), jnp.where(low, got, params)], axis=1)
    return tuple(n.reshape(own, width) for n in news) + (params.reshape(rows, width),)


def solution(mesh):
    placed = (
        P(("section", "pair"), "dp", None, None),
        P(("section", "pair", "dp"), None),
        P(("section", "pair", "dp"), None),
        P(("section", "pair", "dp"), None),
        P("section"),
    )
    return jax.shard_map(
        per_device,
        mesh=mesh,
        in_specs=placed,
        out_specs=(
            P(("section", "pair", "dp"), None),
            P(("section", "pair", "dp"), None),
            P(("section", "pair", "dp"), None),
            P("section", None),
        ),
        check_vma=False,
    )
```

```python
import functools
import math

import jax
import jax.numpy as jnp
from jax import lax
from jax.experimental import pallas as pl
from jax.experimental.pallas import tpu as pltpu
from jax.sharding import PartitionSpec as P

GROUP = ("pair", "dp")
LANES = 128
PARTS = 4


def send(array, bits, core_1_bits=None):
    size = lax.axis_size(GROUP)
    flip = (bits, bits if core_1_bits is None else core_1_bits)
    return lax.ppermute(array, GROUP, [(i, i ^ flip[i & 1]) for i in range(size)])


def row_at(row, tiles, rows):
    sub = min(8, rows)
    return pl.ds((row // sub) * (tiles * sub) + row % sub, tiles, stride=sub)


def place(slot, other):
    pair, shard = lax.axis_index("pair"), lax.axis_index("dp")
    core, near = shard & 1, (shard >> 1) & 1
    return pair ^ (slot * (1 - core)) ^ (other * core), near ^ (slot * core) ^ (other * (1 - core))


def my_rows(shards, own, tiles):
    core, i = lax.axis_index("dp") & 1, 0
    for slot in range(2):
        kept, given = place(slot, 0), place(slot, 1)
        for far in range(shards // 4):
            for o in range(own):
                yield pl.ds(i * tiles, tiles), [
                    (pair * shards + far * 4 + near * 2 + core) * own + o for pair, near in (kept, given)
                ]
                i += 1


def front_kernel(dims, local, master, moment, second, keep_ref, give_ref, state_ref, sems):
    size, tiles, sub = master.shape[0], dims[2], local.shape[1]
    copies = []
    for i, source in enumerate((master, moment, second)):
        copies.append((source, state_ref.at[pl.ds(i * size, size)]))
    for to, rows in my_rows(*dims):
        for row, out_ref in zip(rows, (keep_ref, give_ref)):
            block = pl.ds((row // sub) * tiles, tiles)
            copies.append((local.at[block, row % sub], out_ref.at[to]))
    copies = [pltpu.make_async_copy(*c, sems.at[i]) for i, c in enumerate(copies)]
    for copy in copies:
        copy.start()
    for copy in copies:
        copy.wait()


def sum_kernel(dims, theirs, own_keep, own_give, cross_ref, near_ref, level_ref, keep_ref):
    tiles, rows = dims[2], 2 * dims[0] * dims[1]
    for to, (kept, given) in my_rows(*dims):
        keep = own_keep[to, :] + theirs[row_at(kept, tiles, rows), :]
        keep_ref[to, :] = keep
        level_ref[to, :] = keep
        give = own_give[to, :] + theirs[row_at(given, tiles, rows), :]
        cross_ref[to, :] = give
        near_ref[to, :] = give


def adam(total, master, moment, second, count):
    new_moment = 0.9 * moment + 0.1 * total
    new_second = 0.95 * second + 0.05 * total * total
    first_fix = 1.0 - jnp.exp(count * jnp.log(jnp.full_like(count, 0.9)))
    second_fix = 1.0 - jnp.exp(count * jnp.log(jnp.full_like(count, 0.95)))
    update = new_moment / first_fix / (jnp.sqrt(new_second / second_fix) + 1e-08) + 0.1 * master
    return master - 0.03 * update, new_moment, new_second


def totals(size, sums):
    cross, near, level, keep = (s[...] for s in sums)
    flip = lambda rows: (rows[size:], rows[:size])
    return [
        (c + n) + (l + k)
        for c, n, l, k in zip(flip(cross), flip(near)[::-1], flip(level), flip(keep)[::-1])
    ]


def thirds(size, ref):
    return [ref[i * size:(i + 1) * size, :] for i in range(3)]


def params_kernel(size, step_ref, cross, near, level, keep, state, theirs_state, out_ref):
    count = jnp.full((1, LANES), step_ref[0], jnp.int32).astype(jnp.float32)
    mine, theirs = totals(size, (cross, near, level, keep))
    a, _, _ = adam(mine, *thirds(size, state), count)
    b, _, _ = adam(theirs, *thirds(size, theirs_state), count)
    out_ref[...] = jnp.concatenate([a, b], axis=0).astype(out_ref.dtype)


def own_kernel(size, step_ref, cross, near, level, keep, state, m_ref, v_ref, s_ref):
    count = jnp.full((1, LANES), step_ref[0], jnp.int32).astype(jnp.float32)
    mine, _ = totals(size, (cross, near, level, keep))
    m_ref[...], v_ref[...], s_ref[...] = adam(mine, *thirds(size, state), count)


def order_kernel(own, tiles, *refs):
    pieces, (out_ref, scratch, ready, sems) = refs[:4], refs[4:]
    pair, shard = lax.axis_index("pair"), lax.axis_index("dp")
    core, near = shard & 1, (shard >> 1) & 1
    sources = (
        (pair ^ (1 - core), near ^ core, core ^ 1),
        (pair ^ core, near ^ (1 - core), core),
        (pair, near, core ^ 1),
        (pair, near, core),
    )
    for ref, (p, n, c) in zip(pieces, sources):
        piece = ref[...].astype(jnp.float32)
        for slot in range(2):
            for o in range(own):
                row = ((p ^ (slot * (1 - c))) * 4 + (n ^ (slot * c)) * 2 + c) * own + o
                start = (slot * own + o) * tiles
                scratch[row_at(row, tiles, 8 * own), :] = piece[start:start + tiles]
    part = scratch.shape[0] // PARTS
    copies = []
    for i in range(PARTS):
        at = pl.ds(i * part, part)
        ready[at, :] = scratch[at, :].astype(ready.dtype)
        copies.append(pltpu.make_async_copy(ready.at[at], out_ref.at[at], sems.at[i]))
        copies[i].start()
    for copy in copies:
        copy.wait()


def call(body, outs, *args, hbm=False, out_hbm=False, scratch=()):
    space, out_space = (pltpu.HBM if h else pltpu.VMEM for h in (hbm, out_hbm))
    specs = [pl.BlockSpec(memory_space=pltpu.SMEM if a.dtype == jnp.int32 else space) for a in args]
    held = sum(math.prod(a.shape) * a.dtype.itemsize for a in [*args, *jax.tree.leaves(outs)])
    return pl.pallas_call(
        body,
        out_shape=outs,
        in_specs=specs,
        out_specs=jax.tree.map(lambda _: pl.BlockSpec(memory_space=out_space), outs),
        scratch_shapes=list(scratch),
        compiler_params=pltpu.CompilerParams(vmem_limit_bytes=4 * held + (1 << 20)),
    )(*args)


def per_device(grads, master, moment, second, step):
    rows, width = grads.shape[2], grads.shape[3]
    own, tiles = master.shape[0], width // LANES
    shards = lax.axis_size("dp")
    shard = lax.axis_index("dp")
    far = [1 << b for b in range(2, (shards - 1).bit_length())]
    size, f32 = own * tiles, jnp.float32
    shaped = jax.ShapeDtypeStruct

    master, moment, second = (a.reshape(size, LANES) for a in (master, moment, second))
    sub = min(8, rows)
    local = grads.reshape(rows // sub, sub, tiles, LANES).transpose(0, 2, 1, 3).reshape(rows * tiles, LANES)

    dims = (shards, own, tiles)
    theirs = send(local, 1)
    half = shaped((shards // 2 * size, LANES), f32)
    blocks = local.reshape(rows // sub * tiles, sub, 1, LANES)
    flat = [a.reshape(size, 1, LANES) for a in (master, moment, second)]
    picked = shaped((half.shape[0], 1, LANES), f32)
    keep, give, state = (a.reshape(-1, LANES) for a in call(
        functools.partial(front_kernel, dims), (picked, picked, shaped((3 * size, 1, LANES), f32)),
        *(pltpu.with_memory_space_constraint(a, pltpu.HBM) for a in (blocks, *flat)), hbm=True,
        scratch=[pltpu.SemaphoreType.DMA((3 + 2 * (half.shape[0] // tiles),))]))
    theirs_state = send(state, shards, 2)
    to_cross, to_near, to_level, keep = call(functools.partial(sum_kernel, dims), (half, half, half, half), theirs, keep, give)

    for bit in reversed(far):
        low = (shard & bit) == 0
        held = jnp.stack([keep, to_near]).reshape(2, 2, 2, -1, LANES)
        mine = jnp.where(low, held[:, :, 0], held[:, :, 1])
        other = jnp.where(low, held[:, :, 1], held[:, :, 0])
        keep, to_near = (mine + send(other, bit)).reshape(2, -1, LANES)
        to_cross, to_level = to_near, keep

    cross, near, level = send(to_cross, shards | 2), send(to_near, 2, shards), send(to_level, shards, 2)
    sums = (cross, near, level, keep)

    params = call(
        functools.partial(params_kernel, size), shaped((2 * size, LANES), jnp.bfloat16),
        step, *sums, state, theirs_state)
    row = shaped((size, LANES), f32)
    news = call(
        functools.partial(own_kernel, size), (row, row, row), step, *sums, state)

    pieces = [send(params, 3, shards | 1), send(params, 2, shards), send(params, 1), params]
    block, sub = 8 * own, min(8, 8 * own)
    params = call(
        functools.partial(order_kernel, own, tiles), shaped((block * tiles, LANES), jnp.bfloat16),
        *pieces, out_hbm=True, scratch=[
            pltpu.VMEM((block * tiles, LANES), f32), pltpu.VMEM((block * tiles, LANES), jnp.bfloat16),
            pltpu.SemaphoreType.DMA((PARTS,))])
    params = params.reshape(block // sub, tiles, sub, LANES).transpose(0, 2, 1, 3).reshape(2, 4 * own, width)
    for bit in far:
        low, got = (shard & bit) == 0, send(params, bit)
        params = jnp.concatenate([jnp.where(low, params, got), jnp.where(low, got, params)], axis=1)
    return tuple(n.reshape(own, width) for n in news) + (params.reshape(rows, width),)


def solution(mesh):
    placed = (
        P(("section", "pair"), "dp", None, None),
        P(("section", "pair", "dp"), None),
        P(("section", "pair", "dp"), None),
        P(("section", "pair", "dp"), None),
        P("section"),
    )
    return jax.shard_map(
        per_device,
        mesh=mesh,
        in_specs=placed,
        out_specs=(
            P(("section", "pair", "dp"), None),
            P(("section", "pair", "dp"), None),
            P(("section", "pair", "dp"), None),
            P("section", None),
        ),
        check_vma=False,
    )
```

```python
import functools
import math

import jax
import jax.numpy as jnp
from jax import lax
from jax.experimental import pallas as pl
from jax.experimental.pallas import tpu as pltpu
from jax.sharding import PartitionSpec as P

GROUP = ("pair", "dp")
LANES = 128


def send(array, bits, core_1_bits=None):
    size = lax.axis_size(GROUP)
    flip = (bits, bits if core_1_bits is None else core_1_bits)
    return lax.ppermute(array, GROUP, [(i, i ^ flip[i & 1]) for i in range(size)])


def row_at(row, tiles, rows):
    sub = min(8, rows)
    return pl.ds((row // sub) * (tiles * sub) + row % sub, tiles, stride=sub)


def place(slot, other):
    pair, shard = lax.axis_index("pair"), lax.axis_index("dp")
    core, near = shard & 1, (shard >> 1) & 1
    return pair ^ (slot * core) ^ (other * (1 - core)), near ^ (slot * (1 - core)) ^ (other * core)


def my_rows(shards, own, tiles):
    core, i = lax.axis_index("dp") & 1, 0
    for slot in range(2):
        kept, given = place(slot, 0), place(slot, 1)
        for far in range(shards // 4):
            for o in range(own):
                yield pl.ds(i * tiles, tiles), [
                    (pair * shards + far * 4 + near * 2 + core) * own + o for pair, near in (kept, given)
                ]
                i += 1


def front_kernel(dims, local, master, moment, second, keep_ref, give_ref, state_ref, sems):
    size, tiles, sub = master.shape[0], dims[2], local.shape[1]
    copies = []
    for i, source in enumerate((master, moment, second)):
        copies.append((source, state_ref.at[pl.ds(i * size, size)]))
    for to, rows in my_rows(*dims):
        for row, out_ref in zip(rows, (keep_ref, give_ref)):
            block = pl.ds((row // sub) * tiles, tiles)
            copies.append((local.at[block, row % sub], out_ref.at[to]))
    copies = [pltpu.make_async_copy(*c, sems.at[i]) for i, c in enumerate(copies)]
    for copy in copies:
        copy.start()
    for copy in copies:
        copy.wait()


def sum_kernel(dims, theirs, own_keep, own_give, cross_ref, near_ref, level_ref, keep_ref):
    tiles, rows = dims[2], 2 * dims[0] * dims[1]
    for to, (kept, given) in my_rows(*dims):
        keep = own_keep[to, :] + theirs[row_at(kept, tiles, rows), :]
        keep_ref[to, :] = keep
        level_ref[to, :] = keep
        give = own_give[to, :] + theirs[row_at(given, tiles, rows), :]
        cross_ref[to, :] = give
        near_ref[to, :] = give


def adam(total, master, moment, second, count):
    new_moment = 0.9 * moment + 0.1 * total
    new_second = 0.95 * second + 0.05 * total * total
    first_fix = 1.0 - jnp.exp(count * jnp.log(jnp.full_like(count, 0.9)))
    second_fix = 1.0 - jnp.exp(count * jnp.log(jnp.full_like(count, 0.95)))
    update = new_moment / first_fix / (jnp.sqrt(new_second / second_fix) + 1e-08) + 0.1 * master
    return master - 0.03 * update, new_moment, new_second


def totals(size, sums):
    cross, near, level, keep = (s[...] for s in sums)
    flip = lambda rows: (rows[size:], rows[:size])
    return [
        (c + n) + (l + k)
        for c, n, l, k in zip(flip(cross), flip(near)[::-1], flip(level), flip(keep)[::-1])
    ]


def thirds(size, ref):
    return [ref[i * size:(i + 1) * size, :] for i in range(3)]


def params_kernel(size, step_ref, cross, near, level, keep, state, theirs_state, out_ref):
    count = jnp.full((1, LANES), step_ref[0], jnp.int32).astype(jnp.float32)
    mine, theirs = totals(size, (cross, near, level, keep))
    a, _, _ = adam(mine, *thirds(size, state), count)
    b, _, _ = adam(theirs, *thirds(size, theirs_state), count)
    out_ref[...] = jnp.concatenate([a, b], axis=0).astype(out_ref.dtype)


def own_kernel(size, step_ref, cross, near, level, keep, state, m_ref, v_ref, s_ref):
    count = jnp.full((1, LANES), step_ref[0], jnp.int32).astype(jnp.float32)
    mine, _ = totals(size, (cross, near, level, keep))
    m_ref[...], v_ref[...], s_ref[...] = adam(mine, *thirds(size, state), count)


def order_kernel(own, tiles, *refs):
    pieces, out_ref, scratch = refs[:4], refs[4], refs[5]
    pair, shard = lax.axis_index("pair"), lax.axis_index("dp")
    core, near = shard & 1, (shard >> 1) & 1
    sources = (
        (pair ^ core, near ^ (1 - core), core ^ 1),
        (pair ^ (1 - core), near ^ core, core),
        (pair, near, core ^ 1),
        (pair, near, core),
    )
    for ref, (p, n, c) in zip(pieces, sources):
        piece = ref[...].astype(jnp.float32)
        for slot in range(2):
            for o in range(own):
                row = ((p ^ (slot * c)) * 4 + (n ^ (slot * (1 - c))) * 2 + c) * own + o
                start = (slot * own + o) * tiles
                scratch[row_at(row, tiles, 8 * own), :] = piece[start:start + tiles]
    out_ref[...] = scratch[...].astype(out_ref.dtype)


def call(body, outs, *args, hbm=False, scratch=()):
    space = pltpu.HBM if hbm else pltpu.VMEM
    specs = [pl.BlockSpec(memory_space=pltpu.SMEM if a.dtype == jnp.int32 else space) for a in args]
    held = sum(math.prod(a.shape) * a.dtype.itemsize for a in [*args, *jax.tree.leaves(outs)])
    return pl.pallas_call(
        body,
        out_shape=outs,
        in_specs=specs,
        out_specs=jax.tree.map(lambda _: pl.BlockSpec(memory_space=pltpu.VMEM), outs),
        scratch_shapes=list(scratch),
        compiler_params=pltpu.CompilerParams(vmem_limit_bytes=4 * held + (1 << 20)),
    )(*args)


def per_device(grads, master, moment, second, step):
    rows, width = grads.shape[2], grads.shape[3]
    own, tiles = master.shape[0], width // LANES
    shards = lax.axis_size("dp")
    shard = lax.axis_index("dp")
    far = [1 << b for b in range(2, (shards - 1).bit_length())]
    size, f32 = own * tiles, jnp.float32
    shaped = jax.ShapeDtypeStruct

    master, moment, second = (a.reshape(size, LANES) for a in (master, moment, second))
    sub = min(8, rows)
    local = grads.reshape(rows // sub, sub, tiles, LANES).transpose(0, 2, 1, 3).reshape(rows * tiles, LANES)

    dims = (shards, own, tiles)
    theirs = send(local, 1)
    half = shaped((shards // 2 * size, LANES), f32)
    blocks = local.reshape(rows // sub * tiles, sub, 1, LANES)
    flat = [a.reshape(size, 1, LANES) for a in (master, moment, second)]
    picked = shaped((half.shape[0], 1, LANES), f32)
    keep, give, state = (a.reshape(-1, LANES) for a in call(
        functools.partial(front_kernel, dims), (picked, picked, shaped((3 * size, 1, LANES), f32)),
        *(pltpu.with_memory_space_constraint(a, pltpu.HBM) for a in (blocks, *flat)), hbm=True,
        scratch=[pltpu.SemaphoreType.DMA((3 + 2 * (half.shape[0] // tiles),))]))
    theirs_state = send(state, 2, shards)
    to_cross, to_near, to_level, keep = call(functools.partial(sum_kernel, dims), (half, half, half, half), theirs, keep, give)

    for bit in reversed(far):
        low = (shard & bit) == 0
        held = jnp.stack([keep, to_near]).reshape(2, 2, 2, -1, LANES)
        mine = jnp.where(low, held[:, :, 0], held[:, :, 1])
        other = jnp.where(low, held[:, :, 1], held[:, :, 0])
        keep, to_near = (mine + send(other, bit)).reshape(2, -1, LANES)
        to_cross, to_level = to_near, keep

    cross, near, level = send(to_cross, shards | 2), send(to_near, shards, 2), send(to_level, 2, shards)
    sums = (cross, near, level, keep)

    params = call(
        functools.partial(params_kernel, size), shaped((2 * size, LANES), jnp.bfloat16),
        step, *sums, state, theirs_state)
    row = shaped((size, LANES), f32)
    news = call(
        functools.partial(own_kernel, size), (row, row, row), step, *sums, state)

    pieces = [send(params, shards | 1, 3), send(params, shards, 2), send(params, 1), params]
    block, sub = 8 * own, min(8, 8 * own)
    params = call(
        functools.partial(order_kernel, own, tiles), shaped((block * tiles, LANES), jnp.bfloat16),
        *pieces, scratch=[pltpu.VMEM((block * tiles, LANES), f32)])
    params = params.reshape(block // sub, tiles, sub, LANES).transpose(0, 2, 1, 3).reshape(2, 4 * own, width)
    for bit in far:
        low, got = (shard & bit) == 0, send(params, bit)
        params = jnp.concatenate([jnp.where(low, params, got), jnp.where(low, got, params)], axis=1)
    return tuple(n.reshape(own, width) for n in news) + (params.reshape(rows, width),)


def solution(mesh):
    placed = (
        P(("section", "pair"), "dp", None, None),
        P(("section", "pair", "dp"), None),
        P(("section", "pair", "dp"), None),
        P(("section", "pair", "dp"), None),
        P("section"),
    )
    return jax.shard_map(
        per_device,
        mesh=mesh,
        in_specs=placed,
        out_specs=(
            P(("section", "pair", "dp"), None),
            P(("section", "pair", "dp"), None),
            P(("section", "pair", "dp"), None),
            P("section", None),
        ),
        check_vma=False,
    )
```

```python
import functools
import math

import jax
import jax.numpy as jnp
from jax import lax
from jax.experimental import pallas as pl
from jax.experimental.pallas import tpu as pltpu
from jax.sharding import PartitionSpec as P

GROUP = ("pair", "dp")
LANES = 128


def send(array, bits, core_1_bits=None):
    size = lax.axis_size(GROUP)
    flip = (bits, bits if core_1_bits is None else core_1_bits)
    return lax.ppermute(array, GROUP, [(i, i ^ flip[i & 1]) for i in range(size)])


def row_at(row, tiles, rows):
    sub = min(8, rows)
    return pl.ds((row // sub) * (tiles * sub) + row % sub, tiles, stride=sub)


def place(slot, other):
    pair, shard = lax.axis_index("pair"), lax.axis_index("dp")
    core, near = shard & 1, (shard >> 1) & 1
    return pair ^ (slot * (1 - core)) ^ (other * core), near ^ (slot * core) ^ (other * (1 - core))


def my_rows(shards, own, tiles):
    core, i = lax.axis_index("dp") & 1, 0
    for slot in range(2):
        kept, given = place(slot, 0), place(slot, 1)
        for far in range(shards // 4):
            for o in range(own):
                yield pl.ds(i * tiles, tiles), [
                    (pair * shards + far * 4 + near * 2 + core) * own + o for pair, near in (kept, given)
                ]
                i += 1


def front_kernel(dims, local, master, moment, second, keep_ref, give_ref, state_ref, sems):
    size, tiles, sub = master.shape[0], dims[2], local.shape[1]
    copies = []
    for i, source in enumerate((master, moment, second)):
        copies.append((source, state_ref.at[pl.ds(i * size, size)]))
    for to, rows in my_rows(*dims):
        for row, out_ref in zip(rows, (keep_ref, give_ref)):
            block = pl.ds((row // sub) * tiles, tiles)
            copies.append((local.at[block, row % sub], out_ref.at[to]))
    copies = [pltpu.make_async_copy(*c, sems.at[i]) for i, c in enumerate(copies)]
    for copy in copies:
        copy.start()
    for copy in copies:
        copy.wait()


def sum_kernel(dims, theirs, own_keep, own_give, cross_ref, near_ref, level_ref, keep_ref):
    tiles, rows = dims[2], 2 * dims[0] * dims[1]
    for to, (kept, given) in my_rows(*dims):
        keep = own_keep[to, :] + theirs[row_at(kept, tiles, rows), :]
        keep_ref[to, :] = keep
        level_ref[to, :] = keep
        give = own_give[to, :] + theirs[row_at(given, tiles, rows), :]
        cross_ref[to, :] = give
        near_ref[to, :] = give


def adam(total, master, moment, second, count):
    new_moment = 0.9 * moment + 0.1 * total
    new_second = 0.95 * second + 0.05 * total * total
    first_fix = 1.0 - jnp.exp(count * jnp.log(jnp.full_like(count, 0.9)))
    second_fix = 1.0 - jnp.exp(count * jnp.log(jnp.full_like(count, 0.95)))
    update = new_moment / first_fix / (jnp.sqrt(new_second / second_fix) + 1e-08) + 0.1 * master
    return master - 0.03 * update, new_moment, new_second


def totals(size, sums):
    near, cross, level, keep = (s[...] for s in sums)
    flip = lambda rows: (rows[size:], rows[:size])
    return [
        (c + n) + (l + k)
        for c, n, l, k in zip(flip(cross), flip(near)[::-1], flip(level), flip(keep)[::-1])
    ]


def thirds(size, ref):
    return [ref[i * size:(i + 1) * size, :] for i in range(3)]


def params_kernel(size, step_ref, near, cross, level, keep, state, theirs_state, out_ref):
    count = jnp.full((1, LANES), step_ref[0], jnp.int32).astype(jnp.float32)
    mine, theirs = totals(size, (near, cross, level, keep))
    a, _, _ = adam(mine, *thirds(size, state), count)
    b, _, _ = adam(theirs, *thirds(size, theirs_state), count)
    out_ref[...] = jnp.concatenate([a, b], axis=0).astype(out_ref.dtype)


def own_kernel(size, step_ref, near, cross, level, keep, state, m_ref, v_ref, s_ref):
    count = jnp.full((1, LANES), step_ref[0], jnp.int32).astype(jnp.float32)
    mine, _ = totals(size, (near, cross, level, keep))
    m_ref[...], v_ref[...], s_ref[...] = adam(mine, *thirds(size, state), count)


def order_kernel(own, tiles, *refs):
    pieces, out_ref, scratch = refs[:4], refs[4], refs[5]
    pair, shard = lax.axis_index("pair"), lax.axis_index("dp")
    core, near = shard & 1, (shard >> 1) & 1
    sources = (
        (pair ^ (1 - core), near ^ core, core ^ 1),
        (pair ^ core, near ^ (1 - core), core),
        (pair, near, core ^ 1),
        (pair, near, core),
    )
    for ref, (p, n, c) in zip(pieces, sources):
        piece = ref[...].astype(jnp.float32)
        for slot in range(2):
            for o in range(own):
                row = ((p ^ (slot * (1 - c))) * 4 + (n ^ (slot * c)) * 2 + c) * own + o
                start = (slot * own + o) * tiles
                scratch[row_at(row, tiles, 8 * own), :] = piece[start:start + tiles]
    out_ref[...] = scratch[...].astype(out_ref.dtype)


def call(body, outs, *args, hbm=False, scratch=()):
    space = pltpu.HBM if hbm else pltpu.VMEM
    specs = [pl.BlockSpec(memory_space=pltpu.SMEM if a.dtype == jnp.int32 else space) for a in args]
    held = sum(math.prod(a.shape) * a.dtype.itemsize for a in [*args, *jax.tree.leaves(outs)])
    return pl.pallas_call(
        body,
        out_shape=outs,
        in_specs=specs,
        out_specs=jax.tree.map(lambda _: pl.BlockSpec(memory_space=pltpu.VMEM), outs),
        scratch_shapes=list(scratch),
        compiler_params=pltpu.CompilerParams(vmem_limit_bytes=4 * held + (1 << 20)),
    )(*args)


def per_device(grads, master, moment, second, step):
    rows, width = grads.shape[2], grads.shape[3]
    own, tiles = master.shape[0], width // LANES
    shards = lax.axis_size("dp")
    shard = lax.axis_index("dp")
    far = [1 << b for b in range(2, (shards - 1).bit_length())]
    size, f32 = own * tiles, jnp.float32
    shaped = jax.ShapeDtypeStruct

    master, moment, second = (a.reshape(size, LANES) for a in (master, moment, second))
    sub = min(8, rows)
    local = grads.reshape(rows // sub, sub, tiles, LANES).transpose(0, 2, 1, 3).reshape(rows * tiles, LANES)

    dims = (shards, own, tiles)
    theirs = send(local, 1)
    half = shaped((shards // 2 * size, LANES), f32)
    blocks = local.reshape(rows // sub * tiles, sub, 1, LANES)
    flat = [a.reshape(size, 1, LANES) for a in (master, moment, second)]
    picked = shaped((half.shape[0], 1, LANES), f32)
    keep, give, state = (a.reshape(-1, LANES) for a in call(
        functools.partial(front_kernel, dims), (picked, picked, shaped((3 * size, 1, LANES), f32)),
        *(pltpu.with_memory_space_constraint(a, pltpu.HBM) for a in (blocks, *flat)), hbm=True,
        scratch=[pltpu.SemaphoreType.DMA((3 + 2 * (half.shape[0] // tiles),))]))
    theirs_state = send(state, shards, 2)
    to_cross, to_near, to_level, keep = call(functools.partial(sum_kernel, dims), (half, half, half, half), theirs, keep, give)

    for bit in reversed(far):
        low = (shard & bit) == 0
        held = jnp.stack([keep, to_near]).reshape(2, 2, 2, -1, LANES)
        mine = jnp.where(low, held[:, :, 0], held[:, :, 1])
        other = jnp.where(low, held[:, :, 1], held[:, :, 0])
        keep, to_near = (mine + send(other, bit)).reshape(2, -1, LANES)
        to_cross, to_level = to_near, keep

    cross, near, level = send(to_cross, shards | 2), send(to_near, 2, shards), send(to_level, shards, 2)
    sums = (near, cross, level, keep)

    params = call(
        functools.partial(params_kernel, size), shaped((2 * size, LANES), jnp.bfloat16),
        step, *sums, state, theirs_state)
    row = shaped((size, LANES), f32)
    news = call(
        functools.partial(own_kernel, size), (row, row, row), step, *sums, state)

    pieces = [send(params, 3, shards | 1), send(params, 2, shards), send(params, 1), params]
    block, sub = 8 * own, min(8, 8 * own)
    params = call(
        functools.partial(order_kernel, own, tiles), shaped((block * tiles, LANES), jnp.bfloat16),
        *pieces, scratch=[pltpu.VMEM((block * tiles, LANES), f32)])
    params = params.reshape(block // sub, tiles, sub, LANES).transpose(0, 2, 1, 3).reshape(2, 4 * own, width)
    for bit in far:
        low, got = (shard & bit) == 0, send(params, bit)
        params = jnp.concatenate([jnp.where(low, params, got), jnp.where(low, got, params)], axis=1)
    return tuple(n.reshape(own, width) for n in news) + (params.reshape(rows, width),)


def solution(mesh):
    placed = (
        P(("section", "pair"), "dp", None, None),
        P(("section", "pair", "dp"), None),
        P(("section", "pair", "dp"), None),
        P(("section", "pair", "dp"), None),
        P("section"),
    )
    return jax.shard_map(
        per_device,
        mesh=mesh,
        in_specs=placed,
        out_specs=(
            P(("section", "pair", "dp"), None),
            P(("section", "pair", "dp"), None),
            P(("section", "pair", "dp"), None),
            P("section", None),
        ),
        check_vma=False,
    )
```

```python
import functools
import math

import jax
import jax.numpy as jnp
from jax import lax
from jax.experimental import pallas as pl
from jax.experimental.pallas import tpu as pltpu
from jax.sharding import PartitionSpec as P

GROUP = ("pair", "dp")
LANES = 128


def send(array, bits, core_1_bits=None):
    size = lax.axis_size(GROUP)
    flip = (bits, bits if core_1_bits is None else core_1_bits)
    return lax.ppermute(array, GROUP, [(i, i ^ flip[i & 1]) for i in range(size)])


def row_at(row, tiles, rows):
    sub = min(8, rows)
    return pl.ds((row // sub) * (tiles * sub) + row % sub, tiles, stride=sub)


def place(slot, other):
    pair, shard = lax.axis_index("pair"), lax.axis_index("dp")
    core, near = shard & 1, (shard >> 1) & 1
    return pair ^ (slot * (1 - core)) ^ (other * core), near ^ (slot * core) ^ (other * (1 - core))


def my_rows(shards, own, tiles):
    core, i = lax.axis_index("dp") & 1, 0
    for slot in range(2):
        kept, given = place(slot, 0), place(slot, 1)
        for far in range(shards // 4):
            for o in range(own):
                yield pl.ds(i * tiles, tiles), [
                    (pair * shards + far * 4 + near * 2 + core) * own + o for pair, near in (kept, given)
                ]
                i += 1


def front_kernel(dims, local, master, moment, second, keep_ref, give_ref, state_ref, sems):
    size, tiles, sub = master.shape[0], dims[2], local.shape[1]
    copies = []
    for to, rows in my_rows(*dims):
        for row, out_ref in zip(rows, (keep_ref, give_ref)):
            block = pl.ds((row // sub) * tiles, tiles)
            copies.append((local.at[block, row % sub], out_ref.at[to]))
    for i, source in enumerate((master, moment, second)):
        copies.append((source, state_ref.at[pl.ds(i * size, size)]))
    copies = [pltpu.make_async_copy(*c, sems.at[i]) for i, c in enumerate(copies)]
    for copy in copies:
        copy.start()
    for copy in copies:
        copy.wait()


def sum_kernel(dims, theirs, own_keep, own_give, cross_ref, near_ref, level_ref, keep_ref):
    tiles, rows = dims[2], 2 * dims[0] * dims[1]
    for to, (kept, given) in my_rows(*dims):
        keep = own_keep[to, :] + theirs[row_at(kept, tiles, rows), :]
        keep_ref[to, :] = keep
        level_ref[to, :] = keep
        give = own_give[to, :] + theirs[row_at(given, tiles, rows), :]
        cross_ref[to, :] = give
        near_ref[to, :] = give


def adam(total, master, moment, second, count):
    new_moment = 0.9 * moment + 0.1 * total
    new_second = 0.95 * second + 0.05 * total * total
    first_fix = 1.0 - jnp.exp(count * jnp.log(jnp.full_like(count, 0.9)))
    second_fix = 1.0 - jnp.exp(count * jnp.log(jnp.full_like(count, 0.95)))
    update = new_moment / first_fix / (jnp.sqrt(new_second / second_fix) + 1e-08) + 0.1 * master
    return master - 0.03 * update, new_moment, new_second


def totals(size, sums):
    cross, near, level, keep = (s[...] for s in sums)
    flip = lambda rows: (rows[size:], rows[:size])
    return [
        (c + n) + (l + k)
        for c, n, l, k in zip(flip(cross), flip(near)[::-1], flip(level), flip(keep)[::-1])
    ]


def thirds(size, ref):
    return [ref[i * size:(i + 1) * size, :] for i in range(3)]


def params_kernel(size, step_ref, cross, near, level, keep, state, theirs_state, out_ref):
    count = jnp.full((1, LANES), step_ref[0], jnp.int32).astype(jnp.float32)
    mine, theirs = totals(size, (cross, near, level, keep))
    a, _, _ = adam(mine, *thirds(size, state), count)
    b, _, _ = adam(theirs, *thirds(size, theirs_state), count)
    out_ref[...] = jnp.concatenate([a, b], axis=0).astype(out_ref.dtype)


def own_kernel(size, step_ref, cross, near, level, keep, state, m_ref, v_ref, s_ref):
    count = jnp.full((1, LANES), step_ref[0], jnp.int32).astype(jnp.float32)
    mine, _ = totals(size, (cross, near, level, keep))
    m_ref[...], v_ref[...], s_ref[...] = adam(mine, *thirds(size, state), count)


def order_kernel(own, tiles, *refs):
    pieces, out_ref, scratch = refs[:4], refs[4], refs[5]
    pair, shard = lax.axis_index("pair"), lax.axis_index("dp")
    core, near = shard & 1, (shard >> 1) & 1
    sources = (
        (pair ^ (1 - core), near ^ core, core ^ 1),
        (pair ^ core, near ^ (1 - core), core),
        (pair, near, core ^ 1),
        (pair, near, core),
    )
    for ref, (p, n, c) in zip(pieces, sources):
        piece = ref[...].astype(jnp.float32)
        for slot in range(2):
            for o in range(own):
                row = ((p ^ (slot * (1 - c))) * 4 + (n ^ (slot * c)) * 2 + c) * own + o
                start = (slot * own + o) * tiles
                scratch[row_at(row, tiles, 8 * own), :] = piece[start:start + tiles]
    out_ref[...] = scratch[...].astype(out_ref.dtype)


def call(body, outs, *args, hbm=False, scratch=()):
    space = pltpu.HBM if hbm else pltpu.VMEM
    specs = [pl.BlockSpec(memory_space=pltpu.SMEM if a.dtype == jnp.int32 else space) for a in args]
    held = sum(math.prod(a.shape) * a.dtype.itemsize for a in [*args, *jax.tree.leaves(outs)])
    return pl.pallas_call(
        body,
        out_shape=outs,
        in_specs=specs,
        out_specs=jax.tree.map(lambda _: pl.BlockSpec(memory_space=pltpu.VMEM), outs),
        scratch_shapes=list(scratch),
        compiler_params=pltpu.CompilerParams(vmem_limit_bytes=4 * held + (1 << 20)),
    )(*args)


def per_device(grads, master, moment, second, step):
    rows, width = grads.shape[2], grads.shape[3]
    own, tiles = master.shape[0], width // LANES
    shards = lax.axis_size("dp")
    shard = lax.axis_index("dp")
    far = [1 << b for b in range(2, (shards - 1).bit_length())]
    size, f32 = own * tiles, jnp.float32
    shaped = jax.ShapeDtypeStruct

    master, moment, second = (a.reshape(size, LANES) for a in (master, moment, second))
    sub = min(8, rows)
    local = grads.reshape(rows // sub, sub, tiles, LANES).transpose(0, 2, 1, 3).reshape(rows * tiles, LANES)

    dims = (shards, own, tiles)
    theirs = send(local, 1)
    half = shaped((shards // 2 * size, LANES), f32)
    blocks = local.reshape(rows // sub * tiles, sub, 1, LANES)
    flat = [a.reshape(size, 1, LANES) for a in (master, moment, second)]
    picked = shaped((half.shape[0], 1, LANES), f32)
    keep, give, state = (a.reshape(-1, LANES) for a in call(
        functools.partial(front_kernel, dims), (picked, picked, shaped((3 * size, 1, LANES), f32)),
        *(pltpu.with_memory_space_constraint(a, pltpu.HBM) for a in (blocks, *flat)), hbm=True,
        scratch=[pltpu.SemaphoreType.DMA((3 + 2 * (half.shape[0] // tiles),))]))
    theirs_state = send(state, shards, 2)
    to_cross, to_near, to_level, keep = call(functools.partial(sum_kernel, dims), (half, half, half, half), theirs, keep, give)

    for bit in reversed(far):
        low = (shard & bit) == 0
        held = jnp.stack([keep, to_near]).reshape(2, 2, 2, -1, LANES)
        mine = jnp.where(low, held[:, :, 0], held[:, :, 1])
        other = jnp.where(low, held[:, :, 1], held[:, :, 0])
        keep, to_near = (mine + send(other, bit)).reshape(2, -1, LANES)
        to_cross, to_level = to_near, keep

    cross, near, level = send(to_cross, shards | 2), send(to_near, 2, shards), send(to_level, shards, 2)
    sums = (cross, near, level, keep)

    params = call(
        functools.partial(params_kernel, size), shaped((2 * size, LANES), jnp.bfloat16),
        step, *sums, state, theirs_state)
    row = shaped((size, LANES), f32)
    news = call(
        functools.partial(own_kernel, size), (row, row, row), step, *sums, state)

    pieces = [send(params, 3, shards | 1), send(params, 2, shards), send(params, 1), params]
    block, sub = 8 * own, min(8, 8 * own)
    params = call(
        functools.partial(order_kernel, own, tiles), shaped((block * tiles, LANES), jnp.bfloat16),
        *pieces, scratch=[pltpu.VMEM((block * tiles, LANES), f32)])
    params = params.reshape(block // sub, tiles, sub, LANES).transpose(0, 2, 1, 3).reshape(2, 4 * own, width)
    for bit in far:
        low, got = (shard & bit) == 0, send(params, bit)
        params = jnp.concatenate([jnp.where(low, params, got), jnp.where(low, got, params)], axis=1)
    return tuple(n.reshape(own, width) for n in news) + (params.reshape(rows, width),)


def solution(mesh):
    placed = (
        P(("section", "pair"), "dp", None, None),
        P(("section", "pair", "dp"), None),
        P(("section", "pair", "dp"), None),
        P(("section", "pair", "dp"), None),
        P("section"),
    )
    return jax.shard_map(
        per_device,
        mesh=mesh,
        in_specs=placed,
        out_specs=(
            P(("section", "pair", "dp"), None),
            P(("section", "pair", "dp"), None),
            P(("section", "pair", "dp"), None),
            P("section", None),
        ),
        check_vma=False,
    )
```

```python
import functools
import math

import jax
import jax.numpy as jnp
from jax import lax
from jax.experimental import pallas as pl
from jax.experimental.pallas import tpu as pltpu
from jax.sharding import PartitionSpec as P

GROUP = ("pair", "dp")
LANES = 128


def send(array, bits, core_1_bits=None):
    size = lax.axis_size(GROUP)
    flip = (bits, bits if core_1_bits is None else core_1_bits)
    return lax.ppermute(array, GROUP, [(i, i ^ flip[i & 1]) for i in range(size)])


def row_at(row, tiles, rows):
    sub = min(8, rows)
    return pl.ds((row // sub) * (tiles * sub) + row % sub, tiles, stride=sub)


def place(slot, other):
    pair, shard = lax.axis_index("pair"), lax.axis_index("dp")
    core, near = shard & 1, (shard >> 1) & 1
    return pair ^ (slot * (1 - core)) ^ (other * core), near ^ (slot * core) ^ (other * (1 - core))


def my_rows(shards, own, tiles):
    core, i = lax.axis_index("dp") & 1, 0
    for slot in range(2):
        kept, given = place(slot, 0), place(slot, 1)
        for far in range(shards // 4):
            for o in range(own):
                yield pl.ds(i * tiles, tiles), [
                    (pair * shards + far * 4 + near * 2 + core) * own + o for pair, near in (kept, given)
                ]
                i += 1


def front_kernel(dims, local, master, moment, second, keep_ref, give_ref, state_ref, sems):
    size, tiles, sub = master.shape[0], dims[2], local.shape[1]
    copies = []
    for i, source in enumerate((master, moment, second)):
        copies.append((source, state_ref.at[pl.ds(i * size, size)]))
    for to, rows in my_rows(*dims):
        for row, out_ref in zip(rows, (keep_ref, give_ref)):
            block = pl.ds((row // sub) * tiles, tiles)
            copies.append((local.at[block, row % sub], out_ref.at[to]))
    copies = [pltpu.make_async_copy(*c, sems.at[i]) for i, c in enumerate(copies)]
    for copy in copies:
        copy.start()
    for copy in copies:
        copy.wait()


def sum_kernel(dims, theirs, own_keep, own_give, cross_ref, near_ref, level_ref, keep_ref):
    tiles, rows = dims[2], 2 * dims[0] * dims[1]
    for to, (kept, given) in my_rows(*dims):
        keep = own_keep[to, :] + theirs[row_at(kept, tiles, rows), :]
        keep_ref[to, :] = keep
        level_ref[to, :] = keep
        give = own_give[to, :] + theirs[row_at(given, tiles, rows), :]
        cross_ref[to, :] = give
        near_ref[to, :] = give


def adam(total, master, moment, second, count):
    new_moment = 0.9 * moment + 0.1 * total
    new_second = 0.95 * second + 0.05 * total * total
    first_fix = 1.0 - jnp.exp(count * jnp.log(jnp.full_like(count, 0.9)))
    second_fix = 1.0 - jnp.exp(count * jnp.log(jnp.full_like(count, 0.95)))
    update = new_moment / first_fix / (jnp.sqrt(new_second / second_fix) + 1e-08) + 0.1 * master
    return master - 0.03 * update, new_moment, new_second


def totals(size, sums):
    cross, level, near, keep = (s[...] for s in sums)
    flip = lambda rows: (rows[size:], rows[:size])
    return [
        (c + n) + (l + k)
        for c, n, l, k in zip(flip(cross), flip(near)[::-1], flip(level), flip(keep)[::-1])
    ]


def thirds(size, ref):
    return [ref[i * size:(i + 1) * size, :] for i in range(3)]


def params_kernel(size, step_ref, cross, level, near, keep, state, theirs_state, out_ref):
    count = jnp.full((1, LANES), step_ref[0], jnp.int32).astype(jnp.float32)
    mine, theirs = totals(size, (cross, level, near, keep))
    a, _, _ = adam(mine, *thirds(size, state), count)
    b, _, _ = adam(theirs, *thirds(size, theirs_state), count)
    out_ref[...] = jnp.concatenate([a, b], axis=0).astype(out_ref.dtype)


def own_kernel(size, step_ref, cross, level, near, keep, state, m_ref, v_ref, s_ref):
    count = jnp.full((1, LANES), step_ref[0], jnp.int32).astype(jnp.float32)
    mine, _ = totals(size, (cross, level, near, keep))
    m_ref[...], v_ref[...], s_ref[...] = adam(mine, *thirds(size, state), count)


def order_kernel(own, tiles, *refs):
    pieces, out_ref, scratch = refs[:4], refs[4], refs[5]
    pair, shard = lax.axis_index("pair"), lax.axis_index("dp")
    core, near = shard & 1, (shard >> 1) & 1
    sources = (
        (pair ^ (1 - core), near ^ core, core ^ 1),
        (pair ^ core, near ^ (1 - core), core),
        (pair, near, core ^ 1),
        (pair, near, core),
    )
    for ref, (p, n, c) in zip(pieces, sources):
        piece = ref[...].astype(jnp.float32)
        for slot in range(2):
            for o in range(own):
                row = ((p ^ (slot * (1 - c))) * 4 + (n ^ (slot * c)) * 2 + c) * own + o
                start = (slot * own + o) * tiles
                scratch[row_at(row, tiles, 8 * own), :] = piece[start:start + tiles]
    out_ref[...] = scratch[...].astype(out_ref.dtype)


def call(body, outs, *args, hbm=False, scratch=()):
    space = pltpu.HBM if hbm else pltpu.VMEM
    specs = [pl.BlockSpec(memory_space=pltpu.SMEM if a.dtype == jnp.int32 else space) for a in args]
    held = sum(math.prod(a.shape) * a.dtype.itemsize for a in [*args, *jax.tree.leaves(outs)])
    return pl.pallas_call(
        body,
        out_shape=outs,
        in_specs=specs,
        out_specs=jax.tree.map(lambda _: pl.BlockSpec(memory_space=pltpu.VMEM), outs),
        scratch_shapes=list(scratch),
        compiler_params=pltpu.CompilerParams(vmem_limit_bytes=4 * held + (1 << 20)),
    )(*args)


def per_device(grads, master, moment, second, step):
    rows, width = grads.shape[2], grads.shape[3]
    own, tiles = master.shape[0], width // LANES
    shards = lax.axis_size("dp")
    shard = lax.axis_index("dp")
    far = [1 << b for b in range(2, (shards - 1).bit_length())]
    size, f32 = own * tiles, jnp.float32
    shaped = jax.ShapeDtypeStruct

    master, moment, second = (a.reshape(size, LANES) for a in (master, moment, second))
    sub = min(8, rows)
    local = grads.reshape(rows // sub, sub, tiles, LANES).transpose(0, 2, 1, 3).reshape(rows * tiles, LANES)

    dims = (shards, own, tiles)
    theirs = send(local, 1)
    half = shaped((shards // 2 * size, LANES), f32)
    blocks = local.reshape(rows // sub * tiles, sub, 1, LANES)
    flat = [a.reshape(size, 1, LANES) for a in (master, moment, second)]
    picked = shaped((half.shape[0], 1, LANES), f32)
    keep, give, state = (a.reshape(-1, LANES) for a in call(
        functools.partial(front_kernel, dims), (picked, picked, shaped((3 * size, 1, LANES), f32)),
        *(pltpu.with_memory_space_constraint(a, pltpu.HBM) for a in (blocks, *flat)), hbm=True,
        scratch=[pltpu.SemaphoreType.DMA((3 + 2 * (half.shape[0] // tiles),))]))
    theirs_state = send(state, shards, 2)
    to_cross, to_near, to_level, keep = call(functools.partial(sum_kernel, dims), (half, half, half, half), theirs, keep, give)

    for bit in reversed(far):
        low = (shard & bit) == 0
        held = jnp.stack([keep, to_near]).reshape(2, 2, 2, -1, LANES)
        mine = jnp.where(low, held[:, :, 0], held[:, :, 1])
        other = jnp.where(low, held[:, :, 1], held[:, :, 0])
        keep, to_near = (mine + send(other, bit)).reshape(2, -1, LANES)
        to_cross, to_level = to_near, keep

    cross, near, level = send(to_cross, shards | 2), send(to_near, 2, shards), send(to_level, shards, 2)
    sums = (cross, level, near, keep)

    params = call(
        functools.partial(params_kernel, size), shaped((2 * size, LANES), jnp.bfloat16),
        step, *sums, state, theirs_state)
    row = shaped((size, LANES), f32)
    news = call(
        functools.partial(own_kernel, size), (row, row, row), step, *sums, state)

    pieces = [send(params, 3, shards | 1), send(params, 2, shards), send(params, 1), params]
    block, sub = 8 * own, min(8, 8 * own)
    params = call(
        functools.partial(order_kernel, own, tiles), shaped((block * tiles, LANES), jnp.bfloat16),
        *pieces, scratch=[pltpu.VMEM((block * tiles, LANES), f32)])
    params = params.reshape(block // sub, tiles, sub, LANES).transpose(0, 2, 1, 3).reshape(2, 4 * own, width)
    for bit in far:
        low, got = (shard & bit) == 0, send(params, bit)
        params = jnp.concatenate([jnp.where(low, params, got), jnp.where(low, got, params)], axis=1)
    return tuple(n.reshape(own, width) for n in news) + (params.reshape(rows, width),)


def solution(mesh):
    placed = (
        P(("section", "pair"), "dp", None, None),
        P(("section", "pair", "dp"), None),
        P(("section", "pair", "dp"), None),
        P(("section", "pair", "dp"), None),
        P("section"),
    )
    return jax.shard_map(
        per_device,
        mesh=mesh,
        in_specs=placed,
        out_specs=(
            P(("section", "pair", "dp"), None),
            P(("section", "pair", "dp"), None),
            P(("section", "pair", "dp"), None),
            P("section", None),
        ),
        check_vma=False,
    )
```
